512 devices in a mesh: loop: 16 (over y_lo, x), dp: 16 (over z, core), tensor: 2 (over y_hi).
Axes of the slice: x: 4, y: 8 (y_hi: 2, y_lo: 4; y = y_hi * 4 + y_lo), z: 8, core: 2. Of those that a mesh axis runs over, the one named last changes fastest.
Arguments:
- tokens: bfloat16 [49152, 1024], P(('loop', 'dp')), may hold values from -6 to 6
- expert_ids: int32 [49152, 2], P(('loop', 'dp')), may hold values from 0 to 15, all different within a row; in each aligned block of 192 rows (0 to 191, 192 to 383, ...) at most 36 rows name the same one
- gate_values: float32 [49152, 2], P(('loop', 'dp')), may hold values from 0.2 to 1
- w_gate: bfloat16 [16, 1024, 768], P('loop', None, 'tensor'), may hold values from -0.1875 to 0.1875
- w_up: bfloat16 [16, 1024, 768], P('loop', None, 'tensor'), may hold values from -0.1875 to 0.1875
- w_down: bfloat16 [16, 1024, 768], P('loop', None, 'tensor'), may hold values from -0.21875 to 0.21875
- cotangent: bfloat16 [49152, 1024], P(('loop', 'dp')), may hold values from -24 to 24
Outputs:
- mixed: bfloat16 [49152, 1024], P(('loop', 'dp'), 'tensor')
- token_grad: bfloat16 [49152, 1024], P(('loop', 'dp'), 'tensor')
- grad_gate_w: bfloat16 [16, 1024, 768], P('loop', 'dp', 'tensor')
- grad_up_w: bfloat16 [16, 1024, 768], P('loop', 'dp', 'tensor')
- grad_down_w: bfloat16 [16, 1024, 768], P('loop', 'dp', 'tensor')
The draws below stay inside these ranges and needn't reach their ends.
Inputs may be any that keep to these rules, and one draw needn't show every extreme that they name: `expert_ids`: A row's 2 experts differ. In each aligned block of 192 rows (the rows of one device) no expert is named more than 36 times, a bound that some block reaches.
All inputs are finite; a program needn't handle non-finite values.
Results may differ from the reference program's by a relative error of at most 0.023.
Values may be sent and summed in bfloat16 or wider, within the bound.
No kernel may reach another device: no remote copies, remote signals or barrier semaphores. Data moves between devices by JAX's collectives and lax.ppermute only.
A program may use at most 64 MiB of HBM per device.

```python
import math
import jax
import jax.numpy as jnp
import numpy as np
from jax import lax

D = 1024
FF = 768
TOP = 2
TOK_DEV = 192
EXPERTS = 16
CAP = 36
TOKENS = 49152
N_LOOP = 16
N_DP = 16


def raised(result, key, source, target, blocks, factor):
    owner, partner = [(jnp.arange(result.shape[position]) // (result.shape[position] // blocks)).reshape([-1 if axis == position else 1 for axis in range(result.ndim)]) for position in (source, target)]
    chosen = jax.random.permutation(key, blocks)[partner]
    strong = (owner == chosen) | (owner == (partner + blocks // 2) % blocks)
    return jnp.where(strong, factor * result, result)


def shard_levels(own_key, dims, pieces, smallest, top_value):
    loudness, own = 1.0, jax.random.fold_in(own_key, 6)
    for axis_at, blocks in pieces:
        steps = jnp.exp(jax.random.uniform(jax.random.fold_in(own, axis_at), (blocks,), jnp.float32, smallest / len(pieces), top_value / len(pieces)))
        loudness = loudness * jnp.repeat(steps, dims[axis_at] // blocks).reshape([-1 if axis == axis_at else 1 for axis in range(len(dims))])
    return loudness


def shared_out(key, own, number, rows, count, top, reach, skew):
    order = jax.random.permutation(key, count)
    packed, ordinary = load_shares(count, rows * top, reach, skew, True), load_shares(count, rows * top, reach, skew, False)
    places = jnp.arange(count)

    def named(sizes, offset_by):
        used = int((sizes > 0).sum())
        fixed = max(1, used // 4)
        shifted = fixed + (places - fixed + offset_by * (used - fixed)) % max(1, count - fixed)
        return jnp.zeros((count,), jnp.int32).at[order[jnp.where(places < fixed, places, shifted)]].set(jnp.asarray(sizes, jnp.int32))

    sizes = jnp.where(number % 4 == 0, named(packed, number // 4), named(ordinary, number - number // 4 - 1))
    mixed = jax.random.permutation(jax.random.fold_in(own, 3), count)
    source_of, receiver = mixed[0:count // 2 * 2:2], mixed[1:count // 2 * 2:2]
    margin = jnp.minimum(sizes[source_of] - 1, reach - sizes[receiver]) // 2
    margin = jnp.where((source_of == order[0]) | (receiver == order[0]) | (sizes[receiver] == 0), 0, jnp.maximum(margin, 0))
    shifted = jax.random.randint(jax.random.fold_in(own, 4), (count // 2,), 0, 1 << 20) % (margin + 1)
    sizes = sizes.at[source_of].add(-shifted).at[receiver].add(shifted)
    items = jnp.searchsorted(jnp.cumsum(sizes), jnp.arange(rows * top), side="right").astype(jnp.int32)
    table = items.reshape(top, rows).T
    table = table[jax.random.permutation(jax.random.fold_in(own, 1), rows)]
    offset_by = jax.random.randint(jax.random.fold_in(own, 2), (rows, 1), 0, top)
    return jnp.take_along_axis(table, (jnp.arange(top)[None, :] + offset_by) % top, axis=1)


def load_shares(number_of, total, limit, skew, full):
    portions = [(1 << 20) // math.isqrt(grade ** skew) + 1 for grade in range(1, number_of + 1)]
    largest = limit if full else min(limit, max(-(-total // number_of), total * portions[0] // sum(portions)))
    least = 1 if total - largest >= number_of - 1 else 0
    counts, rest = [largest] + [least] * (number_of - 1), total - largest - least * (number_of - 1)
    while rest > 0:
        free = [i for i in range(1, number_of) if counts[i] < largest] or [i for i in range(1, number_of) if counts[i] < limit]
        mass, remaining = sum([portions[i] for i in free]), rest
        for i in free:
            extra = min(limit - counts[i], max(1, remaining * portions[i] // mass), rest)
            counts[i] = counts[i] + extra
            rest = rest - extra
    return np.array(counts)


def gaussian(key, extent, deviation, bound, shards=(), kind=jnp.bfloat16):
    drawn = jax.random.normal(key, extent, jnp.float32) * deviation
    if len(shards) > 0:
        drawn = shard_levels(key, extent, shards, -0.22, 0.18) * drawn
    return jnp.clip(drawn, min=-bound, max=bound).astype(kind)


def noise_with(own_key, shape, deviation, reach, shards, heavy, kind=jnp.bfloat16):
    drawn = deviation * jax.random.normal(own_key, shape, jnp.float32)
    if shards:
        drawn = drawn * shard_levels(own_key, shape, shards, -0.22, 0.18)
    return jnp.clip(raised(drawn, jax.random.fold_in(own_key, 3), *heavy), -reach, reach).astype(kind)


def setup_inputs(seed: int = 0) -> dict:
    splits = jax.random.split(jax.random.key(seed), 8)
    tokens = gaussian(splits[0], (TOKENS, D), 1.0, 6.0, ((0, 256),))
    expert_ids_keys = jax.random.split(jax.random.fold_in(splits[1], 1), TOKENS // TOK_DEV)
    expert_ids_turns = jax.random.permutation(jax.random.fold_in(splits[1], 3), TOKENS // TOK_DEV)
    expert_ids = jax.vmap(lambda own, number: shared_out(jax.random.fold_in(splits[1], 2), own, number, TOK_DEV, EXPERTS, TOP, CAP, 2))(expert_ids_keys, expert_ids_turns).reshape((TOKENS, TOP))
    gate_values = jnp.clip(0.2 + 0.8 * jax.random.uniform(splits[2], (TOKENS, TOP), jnp.float32) ** shard_levels(splits[2], (TOKENS, TOP), ((0, 256),), -0.2, 0.2), 0.2, 1.0)
    w_gate = gaussian(splits[3], (EXPERTS, D, FF), D ** -0.5, 0.1875, ((0, 16), (2, 2)))
    w_up = gaussian(splits[4], (EXPERTS, D, FF), D ** -0.5, 0.1875, ((0, 16), (2, 2)))
    w_down = gaussian(splits[5], (EXPERTS, D, FF), FF ** -0.5, 0.21875, ((0, 16), (2, 2)))
    cotangent = noise_with(splits[6], (TOKENS, D), 1.0, 24.0, ((0, 256),), (0, 1, 256, 6.0))
    return dict(tokens=tokens, expert_ids=expert_ids, gate_values=gate_values, w_gate=w_gate, w_up=w_up, w_down=w_down, cotangent=cotangent)


def place_slots(flat_ids, experts, capacity):
    onehot = (flat_ids[..., None] == jnp.arange(experts, dtype=jnp.int32)).astype(jnp.int32)
    before = jnp.cumsum(onehot, axis=-2) - onehot
    within = lax.optimization_barrier(jnp.sum(before * onehot, axis=-1))
    return (flat_ids * capacity + within).astype(jnp.int32)

def silu_parts(pre):
    sigma = jax.nn.sigmoid(pre)
    return (pre * sigma, sigma * (1.0 + pre * (1.0 - sigma)))

def expert_pass(rows_in, rows_back, gate_w, up_w, down_w):
    gate_pre = jnp.dot(rows_in, gate_w, preferred_element_type=jnp.float32)
    up_pre = jnp.dot(rows_in, up_w, preferred_element_type=jnp.float32)
    silu_val, silu_slope = silu_parts(gate_pre)
    hidden = (silu_val * up_pre).astype(jnp.bfloat16)
    output = jnp.dot(hidden, down_w.T, preferred_element_type=jnp.float32)
    hidden_grad = jnp.dot(rows_back, down_w, preferred_element_type=jnp.float32)
    gate_grad = (hidden_grad * up_pre * silu_slope).astype(jnp.bfloat16)
    up_grad = (hidden_grad * silu_val).astype(jnp.bfloat16)
    input_grad = jnp.dot(gate_grad, gate_w.T, preferred_element_type=jnp.float32) + jnp.dot(up_grad, up_w.T, preferred_element_type=jnp.float32)
    return (output, input_grad, hidden, gate_grad, up_grad)

def group_grad(left, right):
    left4 = left.reshape(N_LOOP, N_DP, CAP, left.shape[-1]).astype(jnp.float32)
    right4 = right.reshape(N_LOOP, N_DP, CAP, right.shape[-1]).astype(jnp.float32)
    parts = jnp.einsum('ldcx,ldcf->dxf', left4, right4).astype(jnp.bfloat16)
    return lax.optimization_barrier(jnp.sum(parts.astype(jnp.float32), axis=0)).astype(jnp.bfloat16)

def reference(tokens, expert_ids, gate_values, w_gate, w_up, w_down, cotangent):
    blocks = TOKENS // TOK_DEV
    pairs = TOK_DEV * TOP
    flat_ids = expert_ids.reshape(blocks, pairs)
    slots = place_slots(flat_ids, EXPERTS, CAP)
    gate_flat = gate_values.reshape(blocks, pairs, 1).astype(jnp.float32)
    repeated = jnp.repeat(tokens.reshape(blocks, TOK_DEV, D), TOP, axis=1)
    back_rep = jnp.repeat(cotangent.reshape(blocks, TOK_DEV, D), TOP, axis=1)
    weighted = (gate_flat * back_rep.astype(jnp.float32)).astype(jnp.bfloat16)

    def fill(values):

        def one_block(slot_row, value_rows):
            return jnp.zeros((EXPERTS * CAP, D), jnp.bfloat16).at[slot_row].set(value_rows)
        buffers = jax.vmap(one_block)(slots, values)
        return buffers.reshape(blocks, EXPERTS, CAP, D).transpose(1, 0, 2, 3).reshape(EXPERTS, blocks * CAP, D)
    send_rows = fill(repeated)
    send_back = fill(weighted)

    def per_expert(items):
        rows_in, rows_back, gate_w, up_w, down_w = items
        output, input_grad, hidden, gate_grad, up_grad = expert_pass(rows_in, rows_back, gate_w, up_w, down_w)
        return (output, input_grad, group_grad(rows_in, gate_grad), group_grad(rows_in, up_grad), group_grad(rows_back, hidden))
    outputs, input_grads, grad_gate_w, grad_up_w, grad_down_w = lax.map(per_expert, (send_rows, send_back, w_gate, w_up, w_down))

    def take_home(values):
        home = values.reshape(EXPERTS, blocks, CAP, D).transpose(1, 0, 2, 3).reshape(blocks, EXPERTS * CAP, D)
        return jnp.take_along_axis(home, slots[..., None], axis=1)
    home_out = take_home(outputs)
    home_grad = take_home(input_grads)
    mixed = lax.optimization_barrier(jnp.sum((home_out * gate_flat).reshape(blocks, TOK_DEV, TOP, D), axis=2)).reshape(TOKENS, D)
    token_grad = lax.optimization_barrier(jnp.sum(home_grad.reshape(blocks, TOK_DEV, TOP, D), axis=2)).reshape(TOKENS, D)
    return (mixed.astype(jnp.bfloat16), token_grad.astype(jnp.bfloat16), grad_gate_w, grad_up_w, grad_down_w)
```

```python
import functools

import jax
import jax.numpy as jnp
from jax import lax
from jax.experimental import pallas as pl
from jax.experimental.pallas import tpu as pltpu
from jax.sharding import PartitionSpec as P

BF = jnp.bfloat16
F32 = jnp.float32
TOK = 192
D = 1024
HALF = 512
FF = 384
CAP = 36
RUN = 4 * CAP
SLOTS = 16 * CAP
DEVS = 16
GROUP = D // DEVS
VMEM = 40 * 1024 * 1024


def call(body, outs, flops=0, nbytes=0, scratch=()):
    return pl.pallas_call(
        body,
        out_shape=outs,
        scratch_shapes=list(scratch),
        compiler_params=pltpu.CompilerParams(vmem_limit_bytes=VMEM),
        cost_estimate=pl.CostEstimate(flops=flops, bytes_accessed=nbytes, transcendentals=0),
    )


def shape(*dims, dtype=BF):
    return jax.ShapeDtypeStruct(dims, dtype)


def dot(a, b):
    return jnp.dot(a, b, preferred_element_type=F32)


def dot_cols(a, b):
    return lax.dot_general(a, b, (((1,), (1,)), ((), ())), preferred_element_type=F32)


def dot_rows(a, b):
    return lax.dot_general(a, b, (((0,), (0,)), ((), ())), preferred_element_type=F32)


def home_slots(ids, x_major):
    row = lax.axis_index("loop") >> 2
    experts = lax.broadcasted_iota(jnp.int32, (16, TOK), 0)
    named = [experts == ids[k : k + 1, :] for k in range(2)]
    hits = jnp.where(named[0] | named[1], 1.0, 0.0).astype(BF)
    before = jnp.where(
        lax.broadcasted_iota(jnp.int32, (TOK, TOK), 0) < lax.broadcasted_iota(jnp.int32, (TOK, TOK), 1),
        1.0,
        0.0,
    ).astype(BF)
    count = dot(hits, before)
    slots = []
    for k in range(2):
        place = jnp.sum(jnp.where(named[k], count, 0.0), axis=0, keepdims=True)
        expert = ids[k : k + 1, :]
        step = ((expert >> 2) - row) & 3
        column = expert & 3
        block = column * 4 + step if x_major else step * 4 + column
        slots.append(block * CAP + place.astype(jnp.int32))
    return slots


def as_column(row):
    diagonal = lax.broadcasted_iota(jnp.int32, (TOK, TOK), 0) == lax.broadcasted_iota(jnp.int32, (TOK, TOK), 1)
    return jnp.sum(jnp.where(diagonal, row.astype(F32), 0.0), axis=1, keepdims=True)


def store_steps(values, refs):
    for step, ref in ((0, refs[0]), (1, refs[1]), (3, refs[4])):
        ref[...] = values(step).astype(BF)
    rows = values(2)
    refs[2][...] = rows[:, :HALF].astype(BF)
    refs[3][...] = rows[:, HALF:].astype(BF)


STEP_SHAPES = (
    shape(RUN, D),
    shape(RUN, D),
    shape(RUN, HALF),
    shape(RUN, HALF),
    shape(RUN, D),
)


def place_tokens_body(ids_ref, tok_ref, *outs):
    first, second = home_slots(ids_ref[...], False)
    tok = tok_ref[...]

    def values(step):
        slot = lax.broadcasted_iota(jnp.int32, (RUN, TOK), 0) + step * RUN
        pick = jnp.where((slot == first) | (slot == second), 1.0, 0.0).astype(BF)
        return dot(pick, tok)

    store_steps(values, outs)


def place_weighted_body(ids_ref, gate_ref, cot_ref, *outs):
    first, second = home_slots(ids_ref[...], False)
    gates = gate_ref[...]
    cot = cot_ref[...].astype(F32)
    weighted = [(as_column(gates[k : k + 1, :]) * cot).astype(BF) for k in range(2)]

    def values(step):
        slot = lax.broadcasted_iota(jnp.int32, (RUN, TOK), 0) + step * RUN
        return dot(jnp.where(slot == first, 1.0, 0.0).astype(BF), weighted[0]) + dot(
            jnp.where(slot == second, 1.0, 0.0).astype(BF), weighted[1]
        )

    store_steps(values, outs)


def swap_rows(count):
    def block(start):
        row = lax.broadcasted_iota(jnp.int32, (count, SLOTS), 0) + start
        unit = (row * 1821) >> 16
        source = (((unit & 3) << 2) | (unit >> 2)) * CAP + (row - unit * CAP)
        column = lax.broadcasted_iota(jnp.int32, (count, SLOTS), 1)
        return jnp.where(column == source, 1.0, 0.0).astype(BF)

    return block


def turn_body(own_ref, next_ref, left_ref, right_ref, prev_ref, out_ref):
    far = jnp.concatenate([left_ref[...], right_ref[...]], axis=1)
    rows = jnp.concatenate([own_ref[...], next_ref[...], far, prev_ref[...]], axis=0)
    block = swap_rows(RUN)
    for i in range(4):
        out_ref[i] = dot(block(i * RUN), rows).astype(BF)


def forward_body(rows_ref, gate_ref, up_ref, down_ref, gpre_ref, upre_ref, hid_ref, *outs):
    rows = rows_ref[...]
    gate_pre = dot(rows, gate_ref[...])
    up_pre = dot(rows, up_ref[...])
    gpre_ref[...] = gate_pre
    upre_ref[...] = up_pre
    hidden = (gate_pre * jax.nn.sigmoid(gate_pre) * up_pre).astype(BF)
    hid_ref[...] = hidden
    block = swap_rows(RUN)
    down = down_ref[...]
    store_steps(lambda step: dot_cols(dot(block(step * RUN), hidden).astype(BF), down), outs)


def backward_body(back_ref, gpre_ref, upre_ref, gate_ref, up_ref, down_ref, gg_ref, ug_ref, *outs):
    hidden_grad = dot(back_ref[...], down_ref[...])
    gate_pre = gpre_ref[...]
    sigma = jax.nn.sigmoid(gate_pre)
    slope = sigma * (1.0 + gate_pre * (1.0 - sigma))
    gate_grad = (hidden_grad * upre_ref[...] * slope).astype(BF)
    up_grad = (hidden_grad * (gate_pre * sigma)).astype(BF)
    gg_ref[...] = gate_grad
    ug_ref[...] = up_grad
    block = swap_rows(RUN)
    gate, up = gate_ref[...], up_ref[...]

    def values(step):
        pick = block(step * RUN)
        return dot_cols(dot(pick, gate_grad).astype(BF), gate) + dot_cols(dot(pick, up_grad).astype(BF), up)

    store_steps(values, outs)


def weights_body(rows_ref, back_ref, gg_ref, ug_ref, hid_ref, keep_ref, send_ref, all_ref):
    core = lax.axis_index("dp") & 1
    rows, back = rows_ref[...], back_ref[...]
    for i, (left, right) in enumerate(((rows, gg_ref), (rows, ug_ref), (back, hid_ref))):
        term = dot_rows(left, right[...]).astype(BF)
        all_ref[:, :, i * FF : (i + 1) * FF] = term.reshape(DEVS, GROUP, FF)
    for i in range(DEVS // 2):
        keep_ref[i] = all_ref[2 * i + core]
        send_ref[i] = all_ref[2 * i + 1 - core]


def pair_body(keep_ref, got_ref, out_ref):
    out_ref[...] = (keep_ref[...].astype(F32) + got_ref[...].astype(F32)).astype(BF)


def finish_body(parts_ref, gate_ref, up_ref, down_ref):
    total = jnp.sum(parts_ref[...].astype(F32), axis=0).astype(BF)
    gate_ref[0] = total[:, :FF]
    up_ref[0] = total[:, FF : 2 * FF]
    down_ref[0] = total[:, 2 * FF :]


def combine_body(scaled, ids_ref, gate_ref, back_ref, own_ref, send_ref):
    slots = home_slots(ids_ref[...], True)
    column = lax.broadcasted_iota(jnp.int32, (TOK, SLOTS), 1).astype(F32)
    back = back_ref[...]
    if scaled:
        gates = gate_ref[...]
        mix = jnp.zeros((TOK, SLOTS), F32)
        for k in range(2):
            mix = jnp.where(column == as_column(slots[k]), as_column(gates[k : k + 1, :]), mix)
        high = mix.astype(BF)
        low = (mix - high.astype(F32)).astype(BF)
        total = dot(high, back) + dot(low, back)
    else:
        hit = (column == as_column(slots[0])) | (column == as_column(slots[1]))
        total = dot(jnp.where(hit, 1.0, 0.0).astype(BF), back)
    first = lax.axis_index("tensor") == 0
    left, right = total[:, :HALF], total[:, HALF:]
    own_ref[...] = jnp.where(first, left, right)
    send_ref[...] = jnp.where(first, right, left).astype(BF)


def add_body(own_ref, got_ref, out_ref):
    out_ref[...] = (own_ref[...] + got_ref[...].astype(F32)).astype(BF)


def ring(step):
    place = lambda y, x: ((y % 4) * 4 + x) * 2 + y // 4
    return [(place(y, x), place((y + step) % 8, x)) for y in range(8) for x in range(4)]


def along_y(chunks, sign):
    own, one, left, right, three = chunks
    move = lambda value, step: lax.ppermute(value, ("loop", "tensor"), ring((sign * step) % 8))
    left, right = move(left, 2), move(right, -2)
    return own, move(one, 1), left, right, move(three, -1)


def along_x(stack):
    groups = [[4 * y + x for x in range(4)] for y in range(4)]
    moved = lax.all_to_all(stack, "loop", 0, 0, tiled=True, axis_index_groups=groups)
    return moved.reshape(SLOTS, D)


def turned(chunks):
    return call(turn_body, shape(4, RUN, D), 2 * SLOTS * SLOTS * D, 4 * SLOTS * D)(*chunks)


def local(tokens, expert_ids, gate_values, w_gate, w_up, w_down, cotangent):
    ids, gates = expert_ids.T, gate_values.T
    w_gate, w_up, w_down = w_gate[0], w_up[0], w_down[0]
    mm = 2 * SLOTS * D * FF
    tok_steps = call(place_tokens_body, STEP_SHAPES, 2 * SLOTS * TOK * D, 4 * SLOTS * D)(ids, tokens)
    cot_steps = call(place_weighted_body, STEP_SHAPES, 4 * SLOTS * TOK * D, 4 * SLOTS * D)(
        ids, gates, cotangent
    )
    rows = along_x(turned(along_y(tok_steps, 1)))
    back = along_x(turned(along_y(cot_steps, 1)))
    gate_pre, up_pre, hidden, *out_steps = call(
        forward_body,
        (shape(SLOTS, FF, dtype=F32), shape(SLOTS, FF, dtype=F32), shape(SLOTS, FF)) + STEP_SHAPES,
        3 * mm,
        8 * SLOTS * D,
    )(rows, w_gate, w_up, w_down)
    gate_grad, up_grad, *in_steps = call(
        backward_body,
        (shape(SLOTS, FF), shape(SLOTS, FF)) + STEP_SHAPES,
        3 * mm,
        8 * SLOTS * D,
    )(back, gate_pre, up_pre, w_gate, w_up, w_down)
    keep, send = call(
        weights_body,
        (shape(DEVS // 2, GROUP, 3 * FF), shape(DEVS // 2, GROUP, 3 * FF)),
        3 * mm,
        8 * SLOTS * D,
        [pltpu.VMEM((DEVS, GROUP, 3 * FF), BF)],
    )(rows, back, gate_grad, up_grad, hidden)
    home_out = along_x(turned(along_y(out_steps, -1)))
    home_in = along_x(turned(along_y(in_steps, -1)))
    swapped = lax.ppermute(send, "dp", [(i, i ^ 1) for i in range(DEVS)])
    pair = call(pair_body, shape(DEVS // 2, GROUP, 3 * FF), 0, 3 * D * FF * 3)(keep, swapped)
    columns = [[2 * z + core for z in range(DEVS // 2)] for core in range(2)]
    parts = lax.all_to_all(pair, "dp", 0, 0, tiled=True, axis_index_groups=columns)
    grads = call(finish_body, (shape(1, GROUP, FF),) * 3, 0, 3 * D * FF)(parts)
    outs = []
    for scaled, home in ((True, home_out), (False, home_in)):
        own, other = call(
            functools.partial(combine_body, scaled),
            (shape(TOK, HALF, dtype=F32), shape(TOK, HALF)),
            4 * SLOTS * TOK * D,
            4 * SLOTS * D,
        )(ids, gates, home)
        got = lax.ppermute(other, "tensor", [(0, 1), (1, 0)])
        outs.append(call(add_body, shape(TOK, HALF), 0, 8 * TOK * HALF)(own, got))
    return (outs[0], outs[1], *grads)


def solution(mesh):
    spread = P(("loop", "dp"), None)
    weight = P("loop", None, "tensor")
    return jax.shard_map(
        local,
        mesh=mesh,
        in_specs=(spread, spread, spread, weight, weight, weight, spread),
        out_specs=(P(("loop", "dp"), "tensor"),) * 2 + (P("loop", "dp", "tensor"),) * 3,
        check_vma=False,
    )
```

```python
import jax
import jax.numpy as jnp
from jax import lax
from jax.experimental import pallas as pl
from jax.experimental.pallas import tpu as pltpu
from jax.sharding import PartitionSpec as P

BF = jnp.bfloat16
F32 = jnp.float32
TOK = 192
D = 1024
HALF = 512
FF = 384
EXPERTS = 16
MAIN = 32
TAIL = 4
CHUNK = 72
WHOLE = EXPERTS * MAIN
ENDS = EXPERTS * 2 * TAIL
ROWS = WHOLE + ENDS
DEVS = 16
RINGS = 8
GROUP = D // DEVS
VMEM = 56 * 1024 * 1024


def call(body, outs, flops=0, nbytes=0, scratch=()):
    return pl.pallas_call(
        body,
        out_shape=outs,
        scratch_shapes=list(scratch),
        compiler_params=pltpu.CompilerParams(vmem_limit_bytes=VMEM),
        cost_estimate=pl.CostEstimate(flops=flops, bytes_accessed=nbytes, transcendentals=0),
    )


def shape(*dims, dtype=BF):
    return jax.ShapeDtypeStruct(dims, dtype)


def iota(dims, axis):
    return lax.broadcasted_iota(jnp.int32, dims, axis)


def ones_where(condition):
    return jnp.where(condition, 1.0, 0.0).astype(BF)


def dot(a, b):
    return jnp.dot(a, b, preferred_element_type=F32)


def dot_cols(a, b):
    return lax.dot_general(a, b, (((1,), (1,)), ((), ())), preferred_element_type=F32)


def dot_rows(a, b):
    return lax.dot_general(a, b, (((0,), (0,)), ((), ())), preferred_element_type=F32)


def home_places(ids):
    experts = iota((EXPERTS, TOK), 0)
    named = [experts == ids[k : k + 1, :] for k in range(2)]
    before = ones_where(iota((TOK, TOK), 0) < iota((TOK, TOK), 1))
    count = dot(ones_where(named[0] | named[1]), before)
    return [
        (
            ids[k : k + 1, :],
            jnp.sum(jnp.where(named[k], count, 0.0), axis=0, keepdims=True).astype(jnp.int32),
        )
        for k in range(2)
    ]


def as_column(row):
    diagonal = iota((TOK, TOK), 0) == iota((TOK, TOK), 1)
    return jnp.sum(jnp.where(diagonal, row.astype(F32), 0.0), axis=1, keepdims=True)


def place_body(ids_ref, gate_ref, tok_ref, cot_ref, out_ref):
    places = home_places(ids_ref[...])
    gates = gate_ref[...]
    tok = tok_ref[...]
    cot = cot_ref[...].astype(F32)
    weighted = [(as_column(gates[k : k + 1, :]) * cot).astype(BF) for k in range(2)]
    tok_rows = [e * CHUNK + jnp.where(p < MAIN, p, p + MAIN) for e, p in places]
    cot_rows = [r + jnp.where(p < MAIN, MAIN, TAIL) for r, (_, p) in zip(tok_rows, places)]
    for i in range(EXPERTS // 2):
        row = iota((2 * CHUNK, TOK), 0) + i * 2 * CHUNK
        rows = dot(ones_where((row == tok_rows[0]) | (row == tok_rows[1])), tok)
        for k in range(2):
            rows += dot(ones_where(row == cot_rows[k]), weighted[k])
        out_ref[2 * i : 2 * i + 2] = rows.reshape(2, CHUNK, D).astype(BF)


def expert_body(in_ref, gate_ref, up_ref, down_ref, rows_ref, back_ref, gg_ref, ug_ref, hid_ref, out_ref):
    tail = in_ref[:, 2 * MAIN :, :].astype(F32).reshape(ENDS, D)
    row, column = iota((ENDS, ENDS), 0), iota((ENDS, ENDS), 1)
    low = (row & 7) < TAIL
    lift = ones_where(low & (column == row + TAIL))
    lower = ones_where(~low & (column == row - TAIL))
    rows_ref[:WHOLE] = in_ref[:, :MAIN, :].reshape(WHOLE, D)
    rows_ref[WHOLE:] = jnp.where((iota((ENDS, D), 0) & 7) < TAIL, tail, 0.0).astype(BF)
    back_ref[:WHOLE] = in_ref[:, MAIN : 2 * MAIN, :].reshape(WHOLE, D)
    back_ref[WHOLE:] = dot(lift, tail.astype(BF)).astype(BF)
    rows, back = rows_ref[...], back_ref[...]
    gate, up, down = gate_ref[...], up_ref[...], down_ref[...]
    gate_pre = dot(rows, gate)
    up_pre = dot(rows, up)
    hidden_grad = dot(back, down)
    sigma = jax.nn.sigmoid(gate_pre)
    silu = gate_pre * sigma
    hidden = (silu * up_pre).astype(BF)
    gate_grad = (hidden_grad * up_pre * (sigma * (1.0 + gate_pre * (1.0 - sigma)))).astype(BF)
    up_grad = (hidden_grad * silu).astype(BF)
    hid_ref[...] = hidden
    gg_ref[...] = gate_grad
    ug_ref[...] = up_grad
    output = dot_cols(hidden, down)
    input_grad = (dot_cols(gate_grad, gate) + dot_cols(up_grad, up)).astype(BF)
    ends = output[WHOLE:] + dot(lower, input_grad[WHOLE:])
    output = output.astype(BF)
    for h in range(2):
        columns = slice(h * HALF, (h + 1) * HALF)
        out_ref[:, h, :MAIN, :] = output[:WHOLE, columns].reshape(EXPERTS, MAIN, HALF)
        out_ref[:, h, MAIN : 2 * MAIN, :] = input_grad[:WHOLE, columns].reshape(EXPERTS, MAIN, HALF)
        out_ref[:, h, 2 * MAIN :, :] = ends[:, columns].reshape(EXPERTS, 2 * TAIL, HALF).astype(BF)


def weights_body(rows_ref, back_ref, gg_ref, ug_ref, hid_ref, keep_ref, send_ref, all_ref):
    core = lax.axis_index("dp") & 1
    rows, back = rows_ref[...], back_ref[...]
    for i, (left, right) in enumerate(((rows, gg_ref), (rows, ug_ref), (back, hid_ref))):
        term = dot_rows(left, right[...]).astype(BF)
        all_ref[:, :, i * FF : (i + 1) * FF] = term.reshape(DEVS, GROUP, FF)
    for i in range(RINGS):
        keep_ref[i] = all_ref[2 * i + core]
        send_ref[i] = all_ref[2 * i + 1 - core]


def pair_body(keep_ref, got_ref, mine_ref, left_ref, right_ref):
    odd = (lax.axis_index("dp") >> 1) & 1
    for i in range(RINGS // 2):
        j = 2 * i + odd
        mine_ref[i] = (keep_ref[j].astype(F32) + got_ref[j].astype(F32)).astype(BF)
        j = 2 * i + 1 - odd
        other = (keep_ref[j].astype(F32) + got_ref[j].astype(F32)).astype(BF)
        left_ref[i] = other[: GROUP // 2]
        right_ref[i] = other[GROUP // 2 :]


def quarter_body(mine_ref, left_ref, right_ref, own_ref, *outs):
    place = lax.axis_index("dp") >> 2

    def total(i):
        got = jnp.concatenate([left_ref[i], right_ref[i]], axis=0)
        return (mine_ref[i].astype(F32) + got.astype(F32)).astype(BF)

    own_ref[...] = total(place)
    for step, ref in enumerate(outs, 1):
        ref[...] = total((place + step) & 3)


def finish_body(own_ref, one_ref, two_ref, three_ref, gate_ref, up_ref, down_ref):
    total = own_ref[...].astype(F32) + one_ref[...].astype(F32)
    total = (total + two_ref[...].astype(F32) + three_ref[...].astype(F32)).astype(BF)
    gate_ref[0] = total[:, :FF]
    up_ref[0] = total[:, FF : 2 * FF]
    down_ref[0] = total[:, 2 * FF :]


def combine_body(ids_ref, gate_ref, back_ref, mixed_ref, grad_ref):
    places = home_places(ids_ref[...])
    gates = gate_ref[...]
    main_column = iota((TOK, WHOLE), 1).astype(F32)
    tail_column = iota((TOK, ENDS), 1).astype(F32)
    main = [jnp.zeros((TOK, WHOLE), F32)] * 2
    tail = [jnp.zeros((TOK, ENDS), F32)] * 2
    for k, (expert, place) in enumerate(places):
        gate = as_column(gates[k : k + 1, :])
        in_main = main_column == as_column(jnp.where(place < MAIN, expert * MAIN + place, -1))
        at = as_column(jnp.where(place < MAIN, -8, expert * 2 * TAIL + place - MAIN))
        main = [jnp.where(in_main, gate, main[0]), jnp.where(in_main, 1.0, main[1])]
        tail = [jnp.where(tail_column == at, gate, tail[0]), jnp.where(tail_column == at + TAIL, 1.0, tail[1])]

    def split(mix):
        high = mix.astype(BF)
        return high, (mix - high.astype(F32)).astype(BF)

    outs = [jnp.zeros((TOK, HALF), F32)] * 2
    for h in range(2):
        ends = back_ref[:, h, 2 * MAIN :, :].astype(F32).reshape(ENDS, HALF).astype(BF)
        output = back_ref[:, h, :MAIN, :].reshape(WHOLE, HALF)
        input_grad = back_ref[:, h, MAIN : 2 * MAIN, :].reshape(WHOLE, HALF)
        for part, rows in ((main, output), (tail, ends)):
            for piece in split(part[0]):
                outs[0] = outs[0] + dot(piece, rows)
        outs[1] = outs[1] + dot(main[1].astype(BF), input_grad) + dot(tail[1].astype(BF), ends)
    mixed_ref[...] = outs[0].astype(BF)
    grad_ref[...] = outs[1].astype(BF)


def along_z(value, target):
    return lax.ppermute(value, "dp", [(2 * z + core, 2 * (target(z) % RINGS) + core) for z in range(RINGS) for core in range(2)])


def sum_groups(keep, send):
    swapped = lax.ppermute(send, "dp", [(i, i ^ 1) for i in range(DEVS)])
    quarter = shape(RINGS // 2, GROUP // 2, 3 * FF)
    mine, left, right = call(pair_body, (shape(RINGS // 2, GROUP, 3 * FF), quarter, quarter), 0, 9 * D * FF)(
        keep, swapped
    )
    left = along_z(left, lambda z: z ^ 1)
    right = along_z(right, lambda z: z + 1 if z % 2 else z - 1)
    own, *parts = call(quarter_body, (shape(GROUP, 3 * FF),) * 4, 0, 5 * D * FF)(mine, left, right)
    parts = [along_z(part, lambda z, step=step: z + 2 * step) for step, part in enumerate(parts, 1)]
    return call(finish_body, (shape(1, GROUP, FF),) * 3, 0, 2 * D * FF)(own, *parts)


def local(tokens, expert_ids, gate_values, w_gate, w_up, w_down, cotangent):
    ids, gates = expert_ids.T, gate_values.T
    mm = 2 * ROWS * D * FF
    chunks = call(place_body, shape(EXPERTS, CHUNK, D), 4 * mm, 8 * ROWS * D)(ids, gates, tokens, cotangent)
    arrived = lax.all_to_all(chunks, "loop", 0, 0, tiled=True)
    rows, back, gate_grad, up_grad, hidden, results = call(
        expert_body,
        (shape(ROWS, D), shape(ROWS, D)) + (shape(ROWS, FF),) * 3 + (shape(EXPERTS, 2, CHUNK, HALF),),
        6 * mm,
        16 * ROWS * D,
    )(arrived, w_gate[0], w_up[0], w_down[0])
    home = lax.all_to_all(
        results.reshape(2 * EXPERTS, CHUNK, HALF), ("loop", "tensor"), 0, 0, tiled=True
    ).reshape(EXPERTS, 2, CHUNK, HALF)
    keep, send = call(
        weights_body,
        (shape(RINGS, GROUP, 3 * FF), shape(RINGS, GROUP, 3 * FF)),
        3 * mm,
        8 * ROWS * D,
        [pltpu.VMEM((DEVS, GROUP, 3 * FF), BF)],
    )(rows, back, gate_grad, up_grad, hidden)
    grads = sum_groups(keep, send)
    mixed, token_grad = call(combine_body, (shape(TOK, HALF), shape(TOK, HALF)), 2 * mm, 8 * ROWS * D)(
        ids, gates, home
    )
    return (mixed, token_grad, *grads)


def solution(mesh):
    spread = P(("loop", "dp"), None)
    weight = P("loop", None, "tensor")
    return jax.shard_map(
        local,
        mesh=mesh,
        in_specs=(spread, spread, spread, weight, weight, weight, spread),
        out_specs=(P(("loop", "dp"), "tensor"),) * 2 + (P("loop", "dp", "tensor"),) * 3,
        check_vma=False,
    )
```

```python
import jax
import jax.numpy as jnp
from jax import lax
from jax.experimental import pallas as pl
from jax.experimental.pallas import tpu as pltpu
from jax.sharding import PartitionSpec as P

BF = jnp.bfloat16
F32 = jnp.float32
TOK = 192
D = 1024
HALF = 512
FF = 384
EXPERTS = 16
MAIN = 32
TAIL = 4
CHUNK = 72
WHOLE = EXPERTS * MAIN
ENDS = EXPERTS * 2 * TAIL
ROWS = WHOLE + ENDS
DEVS = 16
RINGS = 8
GROUP = D // DEVS
MIB = 1024 * 1024


def call(body, outs, vmem, flops=0, nbytes=0, scratch=(), **specs):
    return pl.pallas_call(
        body,
        out_shape=outs,
        **specs,
        scratch_shapes=list(scratch),
        compiler_params=pltpu.CompilerParams(vmem_limit_bytes=vmem * MIB),
        cost_estimate=pl.CostEstimate(flops=flops, bytes_accessed=nbytes, transcendentals=0),
    )


def shape(*dims, dtype=BF):
    return jax.ShapeDtypeStruct(dims, dtype)


def iota(dims, axis):
    return lax.broadcasted_iota(jnp.int32, dims, axis)


def ones_where(condition):
    return jnp.where(condition, 1.0, 0.0).astype(BF)


def dot(a, b):
    return jnp.dot(a, b, preferred_element_type=F32)


def dot_cols(a, b):
    return lax.dot_general(a, b, (((1,), (1,)), ((), ())), preferred_element_type=F32)


def dot_rows(a, b):
    return lax.dot_general(a, b, (((0,), (0,)), ((), ())), preferred_element_type=F32)


def home_places(ids):
    experts = iota((EXPERTS, TOK), 0)
    named = [experts == ids[k : k + 1, :] for k in range(2)]
    before = ones_where(iota((TOK, TOK), 0) < iota((TOK, TOK), 1))
    count = dot(ones_where(named[0] | named[1]), before)
    return [
        (
            ids[k : k + 1, :],
            jnp.sum(jnp.where(named[k], count, 0.0), axis=0, keepdims=True).astype(jnp.int32),
        )
        for k in range(2)
    ]


def as_column(row):
    diagonal = iota((TOK, TOK), 0) == iota((TOK, TOK), 1)
    return jnp.sum(jnp.where(diagonal, row.astype(F32), 0.0), axis=1, keepdims=True)


def place_body(ids_hbm, gate_hbm, tok_hbm, cot_hbm, out_hbm, out_ref, ids_ref, gate_ref, tok_ref, cot_ref, sems):
    copies = [
        pltpu.make_async_copy(source, target, sems.at[i])
        for i, (source, target) in enumerate(
            ((ids_hbm, ids_ref), (gate_hbm, gate_ref), (cot_hbm, cot_ref), (tok_hbm, tok_ref))
        )
    ]
    for copy in copies:
        copy.start()
    copies[0].wait()
    places = home_places(ids_ref[...])
    tok_rows = [e * CHUNK + jnp.where(p < MAIN, p, p + MAIN) for e, p in places]
    cot_rows = [r + jnp.where(p < MAIN, MAIN, TAIL) for r, (_, p) in zip(tok_rows, places)]
    copies[1].wait()
    gates = [as_column(gate_ref[k : k + 1, :]) for k in range(2)]
    copies[2].wait()
    cot = cot_ref[...].astype(F32)
    weighted = [(gate * cot).astype(BF) for gate in gates]
    copies[3].wait()
    tok = tok_ref[...]
    for i in range(EXPERTS // 2):
        row = iota((2 * CHUNK, TOK), 0) + i * 2 * CHUNK
        rows = dot(ones_where((row == tok_rows[0]) | (row == tok_rows[1])), tok)
        for k in range(2):
            rows += dot(ones_where(row == cot_rows[k]), weighted[k])
        pair = pl.ds(2 * i, 2)
        out_ref[pair] = rows.reshape(2, CHUNK, D).astype(BF)
        copies.append(pltpu.make_async_copy(out_ref.at[pair], out_hbm.at[pair], sems.at[4 + i]))
        copies[-1].start()
    for copy in copies[4:]:
        copy.wait()


def expert_body(
    in_ref, gate_ref, up_ref, down_ref, out_hbm, keep_ref, send_ref, rows_ref, back_ref, out_ref, all_ref, sem
):
    tail = in_ref[:, 2 * MAIN :, :].astype(F32).reshape(ENDS, D)
    row, column = iota((ENDS, ENDS), 0), iota((ENDS, ENDS), 1)
    low = (row & 7) < TAIL
    lift = ones_where(low & (column == row + TAIL))
    lower = ones_where(~low & (column == row - TAIL))
    rows_ref[:WHOLE] = in_ref[:, :MAIN, :].reshape(WHOLE, D)
    rows_ref[WHOLE:] = jnp.where((iota((ENDS, D), 0) & 7) < TAIL, tail, 0.0).astype(BF)
    back_ref[:WHOLE] = in_ref[:, MAIN : 2 * MAIN, :].reshape(WHOLE, D)
    back_ref[WHOLE:] = dot(lift, tail.astype(BF)).astype(BF)
    rows, back = rows_ref[...], back_ref[...]
    gate, up, down = gate_ref[...], up_ref[...], down_ref[...]
    gate_pre = dot(rows, gate)
    up_pre = dot(rows, up)
    hidden_grad = dot(back, down)
    sigma = jax.nn.sigmoid(gate_pre)
    silu = gate_pre * sigma
    hidden = (silu * up_pre).astype(BF)
    gate_grad = (hidden_grad * up_pre * (sigma * (1.0 + gate_pre * (1.0 - sigma)))).astype(BF)
    up_grad = (hidden_grad * silu).astype(BF)
    output = dot_cols(hidden, down)
    input_grad = (dot_cols(gate_grad, gate) + dot_cols(up_grad, up)).astype(BF)
    ends = output[WHOLE:] + dot(lower, input_grad[WHOLE:])
    output = output.astype(BF)
    for h in range(2):
        columns = slice(h * HALF, (h + 1) * HALF)
        out_ref[:, h, :MAIN, :] = output[:WHOLE, columns].reshape(EXPERTS, MAIN, HALF)
        out_ref[:, h, MAIN : 2 * MAIN, :] = input_grad[:WHOLE, columns].reshape(EXPERTS, MAIN, HALF)
        out_ref[:, h, 2 * MAIN :, :] = ends[:, columns].reshape(EXPERTS, 2 * TAIL, HALF).astype(BF)
    copy = pltpu.make_async_copy(out_ref, out_hbm, sem)
    copy.start()
    core = lax.axis_index("dp") & 1
    for i, (left, right) in enumerate(((rows, gate_grad), (rows, up_grad), (back, hidden))):
        term = dot_rows(left, right).astype(BF)
        all_ref[:, :, i * FF : (i + 1) * FF] = term.reshape(DEVS, GROUP, FF)
    for i in range(RINGS):
        keep_ref[i] = all_ref[2 * i + core]
        send_ref[i] = all_ref[2 * i + 1 - core]
    copy.wait()


def pair_body(keep_ref, got_ref, mine_ref, left_ref, right_ref):
    odd = (lax.axis_index("dp") >> 1) & 1
    for i in range(RINGS // 2):
        j = 2 * i + odd
        mine_ref[i] = (keep_ref[j].astype(F32) + got_ref[j].astype(F32)).astype(BF)
        j = 2 * i + 1 - odd
        other = (keep_ref[j].astype(F32) + got_ref[j].astype(F32)).astype(BF)
        left_ref[i] = other[: GROUP // 2]
        right_ref[i] = other[GROUP // 2 :]


def quarter_body(mine_ref, left_ref, right_ref, own_ref, *outs):
    place = lax.axis_index("dp") >> 2

    def total(i):
        got = jnp.concatenate([left_ref[i], right_ref[i]], axis=0)
        return (mine_ref[i].astype(F32) + got.astype(F32)).astype(BF)

    own_ref[...] = total(place)
    for step, ref in enumerate(outs, 1):
        ref[...] = total((place + step) & 3)


def finish_body(own_ref, one_ref, two_ref, three_ref, gate_ref, up_ref, down_ref):
    total = own_ref[...].astype(F32) + one_ref[...].astype(F32)
    total = (total + two_ref[...].astype(F32) + three_ref[...].astype(F32)).astype(BF)
    gate_ref[0] = total[:, :FF]
    up_ref[0] = total[:, FF : 2 * FF]
    down_ref[0] = total[:, 2 * FF :]


def combine_body(ids_ref, gate_ref, back_ref, mixed_ref, grad_ref):
    places = home_places(ids_ref[...])
    gates = gate_ref[...]
    main_column = iota((TOK, WHOLE), 1).astype(F32)
    tail_column = iota((TOK, ENDS), 1).astype(F32)
    main = [jnp.zeros((TOK, WHOLE), F32)] * 2
    tail = [jnp.zeros((TOK, ENDS), F32)] * 2
    for k, (expert, place) in enumerate(places):
        gate = as_column(gates[k : k + 1, :])
        in_main = main_column == as_column(jnp.where(place < MAIN, expert * MAIN + place, -1))
        at = as_column(jnp.where(place < MAIN, -8, expert * 2 * TAIL + place - MAIN))
        main = [jnp.where(in_main, gate, main[0]), jnp.where(in_main, 1.0, main[1])]
        tail = [jnp.where(tail_column == at, gate, tail[0]), jnp.where(tail_column == at + TAIL, 1.0, tail[1])]

    def split(mix):
        high = mix.astype(BF)
        return high, (mix - high.astype(F32)).astype(BF)

    outs = [jnp.zeros((TOK, HALF), F32)] * 2
    for h in range(2):
        ends = back_ref[:, h, 2 * MAIN :, :].astype(F32).reshape(ENDS, HALF).astype(BF)
        output = back_ref[:, h, :MAIN, :].reshape(WHOLE, HALF)
        input_grad = back_ref[:, h, MAIN : 2 * MAIN, :].reshape(WHOLE, HALF)
        for part, rows in ((main, output), (tail, ends)):
            for piece in split(part[0]):
                outs[0] = outs[0] + dot(piece, rows)
        outs[1] = outs[1] + dot(main[1].astype(BF), input_grad) + dot(tail[1].astype(BF), ends)
    mixed_ref[...] = outs[0].astype(BF)
    grad_ref[...] = outs[1].astype(BF)


def runs():
    groups = []
    for dp in range(DEVS):
        for start in (2 * (dp % 2), 2 * (dp % 2) + 4):
            high = {(start + i) % 4: (start + i) % 8 // 4 for i in range(4)}
            groups.append([((4 * y + x) * DEVS + dp) * 2 + high[y] for y in range(4) for x in range(4)])
    return groups


def along_z(value, target):
    return lax.ppermute(value, "dp", [(2 * z + core, 2 * (target(z) % RINGS) + core) for z in range(RINGS) for core in range(2)])


def sum_groups(keep, send):
    swapped = lax.ppermute(send, "dp", [(i, i ^ 1) for i in range(DEVS)])
    quarter = shape(RINGS // 2, GROUP // 2, 3 * FF)
    mine, left, right = call(pair_body, (shape(RINGS // 2, GROUP, 3 * FF), quarter, quarter), 10, 0, 9 * D * FF)(
        keep, swapped
    )
    left = along_z(left, lambda z: z ^ 1)
    right = along_z(right, lambda z: z + 1 if z % 2 else z - 1)
    own, *parts = call(quarter_body, (shape(GROUP, 3 * FF),) * 4, 10, 0, 5 * D * FF)(mine, left, right)
    parts = [along_z(part, lambda z, step=step: z + 2 * step) for step, part in enumerate(parts, 1)]
    return call(finish_body, (shape(1, GROUP, FF),) * 3, 10, 0, 2 * D * FF)(own, *parts)


def local(tokens, expert_ids, gate_values, w_gate, w_up, w_down, cotangent):
    ids, gates = expert_ids.T, gate_values.T
    mm = 2 * ROWS * D * FF
    hbm, vmem = pl.BlockSpec(memory_space=pltpu.HBM), pl.BlockSpec(memory_space=pltpu.VMEM)
    chunks = call(
        place_body,
        shape(EXPERTS, CHUNK, D),
        61,
        4 * mm,
        8 * ROWS * D,
        [
            pltpu.VMEM((EXPERTS, CHUNK, D), BF),
            pltpu.VMEM((2, TOK), jnp.int32),
            pltpu.VMEM((2, TOK), F32),
            pltpu.VMEM((TOK, D), BF),
            pltpu.VMEM((TOK, D), BF),
            pltpu.SemaphoreType.DMA((4 + EXPERTS // 2,)),
        ],
        in_specs=[hbm] * 4,
        out_specs=hbm,
    )(ids, gates, tokens, cotangent)
    arrived = lax.all_to_all(
        chunks, ("loop", "dp", "tensor"), 0, 0, tiled=True, axis_index_groups=runs()
    )
    results, keep, send = call(
        expert_body,
        (shape(EXPERTS, 2, CHUNK, HALF), shape(RINGS, GROUP, 3 * FF), shape(RINGS, GROUP, 3 * FF)),
        58,
        9 * mm,
        16 * ROWS * D,
        [
            pltpu.VMEM((ROWS, D), BF),
            pltpu.VMEM((ROWS, D), BF),
            pltpu.VMEM((EXPERTS, 2, CHUNK, HALF), BF),
            pltpu.VMEM((DEVS, GROUP, 3 * FF), BF),
            pltpu.SemaphoreType.DMA,
        ],
        out_specs=(hbm, vmem, vmem),
    )(arrived, w_gate[0], w_up[0], w_down[0])
    home = lax.all_to_all(
        results.reshape(2 * EXPERTS, CHUNK, HALF), ("loop", "tensor"), 0, 0, tiled=True
    ).reshape(EXPERTS, 2, CHUNK, HALF)
    grads = sum_groups(keep, send)
    mixed, token_grad = call(combine_body, (shape(TOK, HALF), shape(TOK, HALF)), 16, 2 * mm, 8 * ROWS * D)(
        ids, gates, home
    )
    return (mixed, token_grad, *grads)


def solution(mesh):
    spread = P(("loop", "dp"), None)
    weight = P("loop", None, "tensor")
    return jax.shard_map(
        local,
        mesh=mesh,
        in_specs=(spread, spread, spread, weight, weight, weight, spread),
        out_specs=(P(("loop", "dp"), "tensor"),) * 2 + (P("loop", "dp", "tensor"),) * 3,
        check_vma=False,
    )
```

```python
import jax
import jax.numpy as jnp
from jax import lax
from jax.experimental import pallas as pl
from jax.experimental.pallas import tpu as pltpu
from jax.sharding import PartitionSpec as P

BF = jnp.bfloat16
F32 = jnp.float32
TOK = 192
D = 1024
HALF = 512
FF = 384
EXPERTS = 16
MAIN = 32
TAIL = 4
CHUNK = 72
WHOLE = EXPERTS * MAIN
ENDS = EXPERTS * 2 * TAIL
ROWS = WHOLE + ENDS
DEVS = 16
RINGS = 8
GROUP = D // DEVS
MIB = 1024 * 1024


def call(body, outs, vmem, flops=0, nbytes=0, scratch=(), **specs):
    return pl.pallas_call(
        body,
        out_shape=outs,
        **specs,
        scratch_shapes=list(scratch),
        compiler_params=pltpu.CompilerParams(vmem_limit_bytes=int(vmem * MIB)),
        cost_estimate=pl.CostEstimate(flops=flops, bytes_accessed=nbytes, transcendentals=0),
    )


def shape(*dims, dtype=BF):
    return jax.ShapeDtypeStruct(dims, dtype)


def iota(dims, axis):
    return lax.broadcasted_iota(jnp.int32, dims, axis)


def ones_where(condition):
    return jnp.where(condition, 1.0, 0.0).astype(BF)


def dot(a, b):
    return jnp.dot(a, b, preferred_element_type=F32)


def dot_cols(a, b):
    return lax.dot_general(a, b, (((1,), (1,)), ((), ())), preferred_element_type=F32)


def dot_rows(a, b):
    return lax.dot_general(a, b, (((0,), (0,)), ((), ())), preferred_element_type=F32)


def home_places(ids):
    experts = iota((EXPERTS, TOK), 0)
    named = [experts == ids[k : k + 1, :] for k in range(2)]
    before = ones_where(iota((TOK, TOK), 0) < iota((TOK, TOK), 1))
    count = dot(ones_where(named[0] | named[1]), before)
    return [
        (
            ids[k : k + 1, :],
            jnp.sum(jnp.where(named[k], count, 0.0), axis=0, keepdims=True).astype(jnp.int32),
        )
        for k in range(2)
    ]


def as_column(row):
    diagonal = iota((TOK, TOK), 0) == iota((TOK, TOK), 1)
    return jnp.sum(jnp.where(diagonal, row.astype(F32), 0.0), axis=1, keepdims=True)


def place_body(ids_hbm, gate_hbm, tok_hbm, cot_hbm, out_hbm, out_ref, ids_ref, gate_ref, tok_ref, cot_ref, sems):
    copies = [
        pltpu.make_async_copy(source, target, sems.at[i])
        for i, (source, target) in enumerate(
            ((ids_hbm, ids_ref), (gate_hbm, gate_ref), (cot_hbm, cot_ref), (tok_hbm, tok_ref))
        )
    ]
    for copy in copies:
        copy.start()
    copies[0].wait()
    places = home_places(ids_ref[...])
    tok_rows = [e * CHUNK + jnp.where(p < MAIN, p, p + MAIN) for e, p in places]
    cot_rows = [r + jnp.where(p < MAIN, MAIN, TAIL) for r, (_, p) in zip(tok_rows, places)]
    copies[1].wait()
    gates = [as_column(gate_ref[k : k + 1, :]) for k in range(2)]
    def pick(parts, first, span, stride, rows):
        row = iota((rows, TOK), 0)
        slot = (row & (span - 1)) + (row >> (span.bit_length() - 1)) * stride + first
        hit = slot == parts[0]
        for part in parts[1:]:
            hit |= slot == part
        return ones_where(hit)

    copies[2].wait()
    cot = cot_ref[...].astype(F32)
    weighted = [(gate * cot).astype(BF) for gate in gates]
    copies[3].wait()
    tok = tok_ref[...]
    count = EXPERTS // 4
    for i in range(4):
        block = pl.ds(i * count, count)
        start = i * count * CHUNK
        main = dot(pick(tok_rows, start, MAIN, CHUNK, count * MAIN), tok)
        out_ref[block, :MAIN] = main.astype(BF).reshape(count, MAIN, D)
        main = dot(pick(cot_rows[:1], start + MAIN, MAIN, CHUNK, count * MAIN), weighted[0])
        main += dot(pick(cot_rows[1:], start + MAIN, MAIN, CHUNK, count * MAIN), weighted[1])
        out_ref[block, MAIN : 2 * MAIN] = main.astype(BF).reshape(count, MAIN, D)
        ends = dot(pick(tok_rows, start + 2 * MAIN, 2 * TAIL, CHUNK, count * 2 * TAIL), tok)
        for k in range(2):
            ends += dot(pick(cot_rows[k : k + 1], start + 2 * MAIN, 2 * TAIL, CHUNK, count * 2 * TAIL), weighted[k])
        out_ref[block, 2 * MAIN :] = ends.reshape(count, 2 * TAIL, D).astype(BF)
        copies.append(pltpu.make_async_copy(out_ref.at[block], out_hbm.at[block], sems.at[4 + i]))
        copies[-1].start()
    for copy in copies[4:]:
        copy.wait()


def expert_body(in_hbm, gate_ref, up_ref, down_ref, out_hbm, kept_hbm, in_ref, out_ref, kept_ref, sems):
    count, whole, rows = EXPERTS // 2, WHOLE // 2, ROWS // 2
    quarters = [pl.ds(i * EXPERTS // 4, EXPERTS // 4) for i in range(4)]
    loads = [pltpu.make_async_copy(in_hbm.at[q], in_ref.at[q], sems.at[i]) for i, q in enumerate(quarters)]
    for load in loads:
        load.start()
    row, column = iota((ENDS // 2, ENDS // 2), 0), iota((ENDS // 2, ENDS // 2), 1)
    lift = ones_where(((row & 7) < TAIL) & (column == row + TAIL))
    lower = ones_where(((row & 7) >= TAIL) & (column == row - TAIL))
    stores = []

    def send(source, target):
        stores.append(pltpu.make_async_copy(source, target, sems.at[4 + len(stores)]))
        stores[-1].start()

    for part in range(2):
        chunks = pl.ds(part * count, count)
        here, main, last = pl.ds(part * rows, rows), pl.ds(part * rows, whole), pl.ds(part * rows + whole, rows - whole)
        for load in loads[2 * part : 2 * part + 2]:
            load.wait()
        tail = in_ref[chunks, 2 * MAIN :, :].astype(F32).reshape(ENDS // 2, D)
        kept_ref[main, :D] = in_ref[chunks, :MAIN, :].reshape(whole, D)
        kept_ref[last, :D] = jnp.where((iota((ENDS // 2, D), 0) & 7) < TAIL, tail, 0.0).astype(BF)
        kept_ref[main, D : 2 * D] = in_ref[chunks, MAIN : 2 * MAIN, :].reshape(whole, D)
        kept_ref[last, D : 2 * D] = dot(lift, tail.astype(BF)).astype(BF)
        send(kept_ref.at[here, : 2 * D], kept_hbm.at[here, : 2 * D])
        gate_pre = dot(kept_ref[here, :D], gate_ref[...])
        up_pre = dot(kept_ref[here, :D], up_ref[...])
        hidden_grad = dot(kept_ref[here, D : 2 * D], down_ref[...])
        sigma = jax.nn.sigmoid(gate_pre)
        silu = gate_pre * sigma
        gate_grad = (hidden_grad * up_pre * (sigma * (1.0 + gate_pre * (1.0 - sigma)))).astype(BF)
        up_grad = (hidden_grad * silu).astype(BF)
        hidden = (silu * up_pre).astype(BF)
        for i, value in enumerate((gate_grad, up_grad, hidden)):
            kept_ref[here, 2 * D + i * FF : 2 * D + (i + 1) * FF] = value
        send(kept_ref.at[here, 2 * D :], kept_hbm.at[here, 2 * D :])
        for h in range(2):
            columns = pl.ds(h * HALF, HALF)
            output = dot_cols(hidden, down_ref[columns, :])
            input_grad = dot_cols(gate_grad, gate_ref[columns, :]) + dot_cols(up_grad, up_ref[columns, :])
            input_grad = input_grad.astype(BF)
            ends = output[whole:] + dot(lower, input_grad[whole:])
            out_ref[chunks, h, :MAIN, :] = output[:whole].astype(BF).reshape(count, MAIN, HALF)
            out_ref[chunks, h, MAIN : 2 * MAIN, :] = input_grad[:whole].reshape(count, MAIN, HALF)
            out_ref[chunks, h, 2 * MAIN :, :] = ends.reshape(count, 2 * TAIL, HALF).astype(BF)
            send(out_ref.at[chunks, h], out_hbm.at[chunks, h])
    for store in stores:
        store.wait()


def weights_body(kept_hbm, keep_ref, send_ref, kept_ref, all_ref, sems):
    core = lax.axis_index("dp") & 1
    rows, grads = pl.ds(0, D), pl.ds(2 * D, 2 * FF)
    back, hidden = pl.ds(D, D), pl.ds(2 * D + 2 * FF, FF)
    copies = [
        pltpu.make_async_copy(kept_hbm.at[:, part], kept_ref.at[:, part], sems.at[i])
        for i, part in enumerate((rows, grads, back, hidden))
    ]
    for copy in copies:
        copy.start()
    for copy in copies[:2]:
        copy.wait()
    both = dot_rows(kept_ref[:, rows], kept_ref[:, grads]).astype(BF)
    all_ref[:, :, : 2 * FF] = both.reshape(DEVS, GROUP, 2 * FF)
    for copy in copies[2:]:
        copy.wait()
    down = dot_rows(kept_ref[:, back], kept_ref[:, hidden]).astype(BF)
    all_ref[:, :, 2 * FF :] = down.reshape(DEVS, GROUP, FF)
    for i in range(RINGS):
        keep_ref[i] = all_ref[2 * i + core]
        send_ref[i] = all_ref[2 * i + 1 - core]


def pair_body(keep_ref, got_ref, mine_ref, left_ref, right_ref):
    odd = (lax.axis_index("dp") >> 1) & 1
    for i in range(RINGS // 2):
        j = 2 * i + odd
        mine_ref[i] = (keep_ref[j].astype(F32) + got_ref[j].astype(F32)).astype(BF)
        j = 2 * i + 1 - odd
        other = (keep_ref[j].astype(F32) + got_ref[j].astype(F32)).astype(BF)
        left_ref[i] = other[: GROUP // 2]
        right_ref[i] = other[GROUP // 2 :]


def around(z):
    return z + 1 if z % 2 else z - 1


def quarter_body(mine_ref, left_ref, right_ref, own_ref, near_ref, other_ref, far_ref):
    place = lax.axis_index("dp") >> 2

    def total(i):
        got = jnp.concatenate([left_ref[i], right_ref[i]], axis=0)
        return (mine_ref[i].astype(F32) + got.astype(F32)).astype(BF)

    own_ref[...] = total(place)
    near_ref[...] = total(place ^ 1)
    other_ref[...] = total((place + 2 * (place & 1) - 1) & 3)
    far_ref[...] = total(place ^ 2)


def finish_body(own_ref, one_ref, two_ref, three_ref, gate_ref, up_ref, down_ref):
    total = own_ref[...].astype(F32) + one_ref[...].astype(F32)
    total = (total + two_ref[...].astype(F32) + three_ref[...].astype(F32)).astype(BF)
    gate_ref[0] = total[:, :FF]
    up_ref[0] = total[:, FF : 2 * FF]
    down_ref[0] = total[:, 2 * FF :]


def combine_body(ids_ref, gate_ref, back_ref, mixed_ref, grad_ref):
    places = home_places(ids_ref[...])
    gates = gate_ref[...]
    main_column = iota((TOK, WHOLE), 1).astype(F32)
    tail_column = iota((TOK, ENDS), 1).astype(F32)
    main = [jnp.zeros((TOK, WHOLE), F32)] * 2
    tail = [jnp.zeros((TOK, ENDS), F32)] * 2
    for k, (expert, place) in enumerate(places):
        gate = as_column(gates[k : k + 1, :])
        in_main = main_column == as_column(jnp.where(place < MAIN, expert * MAIN + place, -1))
        at = as_column(jnp.where(place < MAIN, -8, expert * 2 * TAIL + place - MAIN))
        main = [jnp.where(in_main, gate, main[0]), jnp.where(in_main, 1.0, main[1])]
        tail = [jnp.where(tail_column == at, gate, tail[0]), jnp.where(tail_column == at + TAIL, 1.0, tail[1])]

    def split(mix):
        high = mix.astype(BF)
        return high, (mix - high.astype(F32)).astype(BF)

    outs = [jnp.zeros((TOK, HALF), F32)] * 2
    for h in range(2):
        ends = back_ref[:, h, 2 * MAIN :, :].astype(F32).reshape(ENDS, HALF).astype(BF)
        output = back_ref[:, h, :MAIN, :].reshape(WHOLE, HALF)
        input_grad = back_ref[:, h, MAIN : 2 * MAIN, :].reshape(WHOLE, HALF)
        for part, rows in ((main, output), (tail, ends)):
            for piece in split(part[0]):
                outs[0] = outs[0] + dot(piece, rows)
        outs[1] = outs[1] + dot(main[1].astype(BF), input_grad) + dot(tail[1].astype(BF), ends)
    mixed_ref[...] = outs[0].astype(BF)
    grad_ref[...] = outs[1].astype(BF)


def runs():
    groups = []
    for dp in range(DEVS):
        for start in (2 * (dp % 2), 2 * (dp % 2) + 4):
            high = {(start + i) % 4: (start + i) % 8 // 4 for i in range(4)}
            groups.append([((4 * y + x) * DEVS + dp) * 2 + high[y] for y in range(4) for x in range(4)])
    return groups


def along_z(value, target):
    return lax.ppermute(value, "dp", [(2 * z + core, 2 * (target(z) % RINGS) + core) for z in range(RINGS) for core in range(2)])


def sum_groups(keep, send):
    swapped = lax.ppermute(send, "dp", [(i, i ^ 1) for i in range(DEVS)])
    quarter = shape(RINGS // 2, GROUP // 2, 3 * FF)
    mine, left, right = call(pair_body, (shape(RINGS // 2, GROUP, 3 * FF), quarter, quarter), 10, 0, 9 * D * FF)(
        keep, swapped
    )
    left = along_z(left, lambda z: z ^ 1)
    right = along_z(right, around)
    own, *parts = call(quarter_body, (shape(GROUP, 3 * FF),) * 4, 10, 0, 5 * D * FF)(mine, left, right)
    targets = (lambda z: z ^ 2, lambda z: 2 * around(z // 2) + z % 2, lambda z: z ^ 4)
    parts = [along_z(part, target) for part, target in zip(parts, targets)]
    return call(finish_body, (shape(1, GROUP, FF),) * 3, 10, 0, 2 * D * FF)(own, *parts)


def local(tokens, expert_ids, gate_values, w_gate, w_up, w_down, cotangent):
    ids, gates = expert_ids.T, gate_values.T
    mm = 2 * ROWS * D * FF
    hbm, vmem = pl.BlockSpec(memory_space=pltpu.HBM), pl.BlockSpec(memory_space=pltpu.VMEM)
    chunks = call(
        place_body,
        shape(EXPERTS, CHUNK, D),
        61,
        4 * mm,
        8 * ROWS * D,
        [
            pltpu.VMEM((EXPERTS, CHUNK, D), BF),
            pltpu.VMEM((2, TOK), jnp.int32),
            pltpu.VMEM((2, TOK), F32),
            pltpu.VMEM((TOK, D), BF),
            pltpu.VMEM((TOK, D), BF),
            pltpu.SemaphoreType.DMA((8,)),
        ],
        in_specs=[hbm] * 4,
        out_specs=hbm,
    )(ids, gates, tokens, cotangent)
    arrived = lax.all_to_all(
        chunks, ("loop", "dp", "tensor"), 0, 0, tiled=True, axis_index_groups=runs()
    )
    kept = shape(ROWS, 2 * D + 3 * FF)
    results, kept = call(
        expert_body,
        (shape(EXPERTS, 2, CHUNK, HALF), kept),
        50,
        6 * mm,
        16 * ROWS * D,
        [
            pltpu.VMEM((EXPERTS, CHUNK, D), BF),
            pltpu.VMEM((EXPERTS, 2, CHUNK, HALF), BF),
            pltpu.VMEM((ROWS, 2 * D + 3 * FF), BF),
            pltpu.SemaphoreType.DMA((12,)),
        ],
        in_specs=[hbm, vmem, vmem, vmem],
        out_specs=(hbm, hbm),
    )(arrived, w_gate[0], w_up[0], w_down[0])
    home = lax.all_to_all(
        results.reshape(2 * EXPERTS, CHUNK, HALF), ("loop", "tensor"), 0, 0, tiled=True
    ).reshape(EXPERTS, 2, CHUNK, HALF)
    keep, send = call(
        weights_body,
        (shape(RINGS, GROUP, 3 * FF), shape(RINGS, GROUP, 3 * FF)),
        50,
        3 * mm,
        8 * ROWS * D,
        [
            pltpu.VMEM((ROWS, 2 * D + 3 * FF), BF),
            pltpu.VMEM((DEVS, GROUP, 3 * FF), BF),
            pltpu.SemaphoreType.DMA((4,)),
        ],
        in_specs=[hbm],
    )(kept)
    grads = sum_groups(keep, send)
    mixed, token_grad = call(combine_body, (shape(TOK, HALF), shape(TOK, HALF)), 16, 2 * mm, 8 * ROWS * D)(
        ids, gates, home
    )
    return (mixed, token_grad, *grads)


def solution(mesh):
    spread = P(("loop", "dp"), None)
    weight = P("loop", None, "tensor")
    return jax.shard_map(
        local,
        mesh=mesh,
        in_specs=(spread, spread, spread, weight, weight, weight, spread),
        out_specs=(P(("loop", "dp"), "tensor"),) * 2 + (P("loop", "dp", "tensor"),) * 3,
        check_vma=False,
    )
```

```python
import jax
import jax.numpy as jnp
from jax import lax
from jax.experimental import pallas as pl
from jax.experimental.pallas import tpu as pltpu
from jax.sharding import PartitionSpec as P

BF = jnp.bfloat16
F32 = jnp.float32
TOK = 192
D = 1024
HALF = 512
FF = 384
EXPERTS = 16
MAIN = 32
TAIL = 4
CHUNK = 72
WHOLE = EXPERTS * MAIN
ENDS = EXPERTS * 2 * TAIL
ROWS = WHOLE + ENDS
DEVS = 16
RINGS = 8
GROUP = D // DEVS
MIB = 1024 * 1024


def call(body, outs, vmem, flops=0, nbytes=0, scratch=(), **specs):
    return pl.pallas_call(
        body,
        out_shape=outs,
        **specs,
        scratch_shapes=list(scratch),
        compiler_params=pltpu.CompilerParams(vmem_limit_bytes=int(vmem * MIB)),
        cost_estimate=pl.CostEstimate(flops=flops, bytes_accessed=nbytes, transcendentals=0),
    )


def shape(*dims, dtype=BF):
    return jax.ShapeDtypeStruct(dims, dtype)


def iota(dims, axis):
    return lax.broadcasted_iota(jnp.int32, dims, axis)


def ones_where(condition):
    return jnp.where(condition, 1.0, 0.0).astype(BF)


def dot(a, b):
    return jnp.dot(a, b, preferred_element_type=F32)


def dot_cols(a, b):
    return lax.dot_general(a, b, (((1,), (1,)), ((), ())), preferred_element_type=F32)


def dot_rows(a, b):
    return lax.dot_general(a, b, (((0,), (0,)), ((), ())), preferred_element_type=F32)


def home_places(ids):
    experts = iota((EXPERTS, TOK), 0)
    named = [experts == ids[k : k + 1, :] for k in range(2)]
    before = ones_where(iota((TOK, TOK), 0) < iota((TOK, TOK), 1))
    count = dot(ones_where(named[0] | named[1]), before)
    return [
        (
            ids[k : k + 1, :],
            jnp.sum(jnp.where(named[k], count, 0.0), axis=0, keepdims=True).astype(jnp.int32),
        )
        for k in range(2)
    ]


def as_column(row):
    diagonal = iota((TOK, TOK), 0) == iota((TOK, TOK), 1)
    return jnp.sum(jnp.where(diagonal, row.astype(F32), 0.0), axis=1, keepdims=True)


def place_body(ids_hbm, gate_hbm, tok_hbm, cot_hbm, out_hbm, out_ref, ids_ref, gate_ref, tok_ref, cot_ref, sems):
    copies = [
        pltpu.make_async_copy(source, target, sems.at[i])
        for i, (source, target) in enumerate(
            ((ids_hbm, ids_ref), (gate_hbm, gate_ref), (cot_hbm, cot_ref), (tok_hbm, tok_ref))
        )
    ]
    for copy in copies:
        copy.start()
    copies[0].wait()
    places = home_places(ids_ref[...])
    tok_rows = [e * CHUNK + jnp.where(p < MAIN, p, p + MAIN) for e, p in places]
    cot_rows = [r + jnp.where(p < MAIN, MAIN, TAIL) for r, (_, p) in zip(tok_rows, places)]
    copies[1].wait()
    gates = [as_column(gate_ref[k : k + 1, :]) for k in range(2)]
    def pick(parts, first, span, stride, rows):
        row = iota((rows, TOK), 0)
        slot = (row & (span - 1)) + (row >> (span.bit_length() - 1)) * stride + first
        hit = slot == parts[0]
        for part in parts[1:]:
            hit |= slot == part
        return ones_where(hit)

    copies[2].wait()
    cot = cot_ref[...].astype(F32)
    weighted = [(gate * cot).astype(BF) for gate in gates]
    copies[3].wait()
    tok = tok_ref[...]
    count = EXPERTS // 2
    for i in range(2):
        block = pl.ds(i * count, count)
        start = i * count * CHUNK
        main = dot(pick(tok_rows, start, MAIN, CHUNK, count * MAIN), tok)
        out_ref[block, :MAIN] = main.astype(BF).reshape(count, MAIN, D)
        main = dot(pick(cot_rows[:1], start + MAIN, MAIN, CHUNK, count * MAIN), weighted[0])
        main += dot(pick(cot_rows[1:], start + MAIN, MAIN, CHUNK, count * MAIN), weighted[1])
        out_ref[block, MAIN : 2 * MAIN] = main.astype(BF).reshape(count, MAIN, D)
        ends = dot(pick(tok_rows, start + 2 * MAIN, 2 * TAIL, CHUNK, count * 2 * TAIL), tok)
        for k in range(2):
            ends += dot(pick(cot_rows[k : k + 1], start + 2 * MAIN, 2 * TAIL, CHUNK, count * 2 * TAIL), weighted[k])
        out_ref[block, 2 * MAIN :] = ends.reshape(count, 2 * TAIL, D).astype(BF)
        copies.append(pltpu.make_async_copy(out_ref.at[block], out_hbm.at[block], sems.at[4 + i]))
        copies[-1].start()
    for copy in copies[4:]:
        copy.wait()


def expert_body(
    in_hbm, gate_ref, up_ref, down_ref, out_hbm, kept_hbm, in_ref, out_ref, kept_ref, rest_ref, sems
):
    quarter = EXPERTS // 4
    quarters = [pl.ds(i * quarter, quarter) for i in range(4)]
    loads = [pltpu.make_async_copy(in_hbm.at[q], in_ref.at[q], sems.at[i]) for i, q in enumerate(quarters)]
    for load in loads:
        load.start()
    row, column = iota((ENDS, ENDS), 0), iota((ENDS, ENDS), 1)
    lift = ones_where(((row & 7) < TAIL) & (column == row + TAIL))
    lower = ones_where(((row & 7) >= TAIL) & (column == row - TAIL))
    stores = []

    def send(source, target):
        stores.append(pltpu.make_async_copy(source, target, sems.at[4 + len(stores)]))
        stores[-1].start()

    wide = 256
    narrow = FF - wide
    rest_ref[:, :narrow] = gate_ref[:, wide:]
    rest_ref[:, narrow:] = up_ref[:, wide:]
    for i, load in enumerate(loads):
        load.wait()
        part = pl.ds(i * quarter * MAIN, quarter * MAIN)
        kept_ref[part, :D] = in_ref[quarters[i], :MAIN, :].reshape(quarter * MAIN, D)
        kept_ref[part, D : 2 * D] = in_ref[quarters[i], MAIN : 2 * MAIN, :].reshape(quarter * MAIN, D)
    tail = in_ref[:, 2 * MAIN :, :].astype(F32).reshape(ENDS, D)
    kept_ref[WHOLE:, :D] = jnp.where((iota((ENDS, D), 0) & 7) < TAIL, tail, 0.0).astype(BF)
    kept_ref[WHOLE:, D : 2 * D] = dot(lift, tail.astype(BF)).astype(BF)
    send(kept_ref.at[:, : 2 * D], kept_hbm.at[:, : 2 * D])
    rows = kept_ref[:, :D]
    rest = dot(rows, rest_ref[...])
    gate_pre = jnp.concatenate([dot(rows, gate_ref[:, :wide]), rest[:, :narrow]], axis=1)
    up_pre = jnp.concatenate([dot(rows, up_ref[:, :wide]), rest[:, narrow:]], axis=1)
    hidden_grad = dot(kept_ref[:, D : 2 * D], down_ref[...])
    sigma = jax.nn.sigmoid(gate_pre)
    silu = gate_pre * sigma
    gate_grad = (hidden_grad * up_pre * (sigma * (1.0 + gate_pre * (1.0 - sigma)))).astype(BF)
    up_grad = (hidden_grad * silu).astype(BF)
    hidden = (silu * up_pre).astype(BF)
    for i, value in enumerate((gate_grad, up_grad, hidden)):
        kept_ref[:, 2 * D + i * FF : 2 * D + (i + 1) * FF] = value
    send(kept_ref.at[:, 2 * D :], kept_hbm.at[:, 2 * D :])
    rest = jnp.concatenate([gate_grad[:, wide:], up_grad[:, wide:]], axis=1)
    for h in range(2):
        part = pl.ds(h * HALF, HALF)
        output = dot_cols(hidden, down_ref[part, :])
        input_grad = dot_cols(gate_grad[:, :wide], gate_ref[part, :wide])
        input_grad += dot_cols(up_grad[:, :wide], up_ref[part, :wide])
        input_grad = (input_grad + dot_cols(rest, rest_ref[part, :])).astype(BF)
        ends = output[WHOLE:] + dot(lower, input_grad[WHOLE:])
        out_ref[:, h, :MAIN, :] = output[:WHOLE].astype(BF).reshape(EXPERTS, MAIN, HALF)
        out_ref[:, h, MAIN : 2 * MAIN, :] = input_grad[:WHOLE].reshape(EXPERTS, MAIN, HALF)
        out_ref[:, h, 2 * MAIN :, :] = ends.reshape(EXPERTS, 2 * TAIL, HALF).astype(BF)
        send(out_ref.at[:, h], out_hbm.at[:, h])
    for store in stores:
        store.wait()


def weights_body(kept_hbm, keep_ref, send_ref, kept_ref, all_ref, sems):
    core = lax.axis_index("dp") & 1
    rows, grads = pl.ds(0, D), pl.ds(2 * D, 2 * FF)
    back, hidden = pl.ds(D, D), pl.ds(2 * D + 2 * FF, FF)
    copies = [
        pltpu.make_async_copy(kept_hbm.at[:, part], kept_ref.at[:, part], sems.at[i])
        for i, part in enumerate((rows, grads, back, hidden))
    ]
    for copy in copies:
        copy.start()
    for copy in copies[:2]:
        copy.wait()
    both = dot_rows(kept_ref[:, rows], kept_ref[:, grads]).astype(BF)
    all_ref[:, :, : 2 * FF] = both.reshape(DEVS, GROUP, 2 * FF)
    for copy in copies[2:]:
        copy.wait()
    down = dot_rows(kept_ref[:, back], kept_ref[:, hidden]).astype(BF)
    all_ref[:, :, 2 * FF :] = down.reshape(DEVS, GROUP, FF)
    for i in range(RINGS):
        keep_ref[i] = all_ref[2 * i + core]
        send_ref[i] = all_ref[2 * i + 1 - core]


def around(z):
    return (z + 2 * (z & 1) - 1) & (RINGS - 1)


def add(left, right):
    return (left.astype(F32) + right.astype(F32)).astype(BF)


def split_body(keep_ref, got_ref, *outs):
    z = lax.axis_index("dp") >> 1
    half = GROUP // 2
    for part, (own, partner, later) in enumerate(((z, around(z), lambda i: i ^ 1), (z, z ^ 1, around))):
        rows = pl.ds(part * half, half)
        for ref, chip in zip(outs[2 * part : 2 * part + 2], (own, partner)):
            for i, chunk in enumerate((chip, chip ^ 4, later(chip), later(chip) ^ 4)):
                ref[i] = add(keep_ref[chunk, rows], got_ref[chunk, rows])


def halve_body(*refs):
    for mine_ref, got_ref, keep_ref, send_ref in (refs[0::2], refs[1::2]):
        half = mine_ref.shape[0] // 2
        keep_ref[...] = add(mine_ref[:half], got_ref[:half])
        send_ref[...] = add(mine_ref[half:], got_ref[half:])


def join_body(mine0_ref, mine1_ref, got0_ref, got1_ref, keep_ref, send_ref):
    half = GROUP // 2
    for part, (mine_ref, got_ref) in enumerate(((mine0_ref, got0_ref), (mine1_ref, got1_ref))):
        rows = pl.ds(part * half, half)
        keep_ref[0, rows] = add(mine_ref[0], got_ref[0])
        send_ref[0, rows] = add(mine_ref[1], got_ref[1])


def finish_body(own_ref, got_ref, gate_ref, up_ref, down_ref):
    total = add(own_ref[...], got_ref[...])
    gate_ref[...] = total[:, :, :FF]
    up_ref[...] = total[:, :, FF : 2 * FF]
    down_ref[...] = total[:, :, 2 * FF :]


def combine_body(ids_ref, gate_ref, back_ref, mixed_ref, grad_ref):
    places = home_places(ids_ref[...])
    gates = gate_ref[...]
    main_column = iota((TOK, WHOLE), 1).astype(F32)
    tail_column = iota((TOK, ENDS), 1).astype(F32)
    main = [jnp.zeros((TOK, WHOLE), F32)] * 2
    tail = [jnp.zeros((TOK, ENDS), F32)] * 2
    for k, (expert, place) in enumerate(places):
        gate = as_column(gates[k : k + 1, :])
        in_main = main_column == as_column(jnp.where(place < MAIN, expert * MAIN + place, -1))
        at = as_column(jnp.where(place < MAIN, -8, expert * 2 * TAIL + place - MAIN))
        main = [jnp.where(in_main, gate, main[0]), jnp.where(in_main, 1.0, main[1])]
        tail = [jnp.where(tail_column == at, gate, tail[0]), jnp.where(tail_column == at + TAIL, 1.0, tail[1])]

    def split(mix):
        high = mix.astype(BF)
        return high, (mix - high.astype(F32)).astype(BF)

    outs = [jnp.zeros((TOK, HALF), F32)] * 2
    for h in range(2):
        ends = back_ref[:, h, 2 * MAIN :, :].astype(F32).reshape(ENDS, HALF).astype(BF)
        output = back_ref[:, h, :MAIN, :].reshape(WHOLE, HALF)
        input_grad = back_ref[:, h, MAIN : 2 * MAIN, :].reshape(WHOLE, HALF)
        for part, rows in ((main, output), (tail, ends)):
            for piece in split(part[0]):
                outs[0] = outs[0] + dot(piece, rows)
        outs[1] = outs[1] + dot(main[1].astype(BF), input_grad) + dot(tail[1].astype(BF), ends)
    mixed_ref[...] = outs[0].astype(BF)
    grad_ref[...] = outs[1].astype(BF)


def runs():
    groups = []
    for dp in range(DEVS):
        for start in (2 * (dp % 2), 2 * (dp % 2) + 4):
            high = {(start + i) % 4: (start + i) % 8 // 4 for i in range(4)}
            groups.append([((4 * y + x) * DEVS + dp) * 2 + high[y] for y in range(4) for x in range(4)])
    return groups


def along_z(value, target):
    return lax.ppermute(value, "dp", [(2 * z + core, 2 * (target(z) % RINGS) + core) for z in range(RINGS) for core in range(2)])


def sum_groups(keep, send):
    some = lambda count: shape(count, GROUP // 2, 3 * FF)
    whole = shape(1, GROUP, 3 * FF)
    got = lax.ppermute(send, "dp", [(i, i ^ 1) for i in range(DEVS)])
    mine0, other0, mine1, other1 = call(split_body, (some(4),) * 4, 10, 0, 12 * D * FF)(keep, got)
    got0, got1 = along_z(other0, around), along_z(other1, lambda z: z ^ 1)
    mine0, mine1, other0, other1 = call(halve_body, (some(2),) * 4, 10, 0, 6 * D * FF)(mine0, mine1, got0, got1)
    got0, got1 = along_z(other0, lambda z: z ^ 1), along_z(other1, around)
    mine, other = call(join_body, (whole, whole), 10, 0, 3 * D * FF)(mine0, mine1, got0, got1)
    got = along_z(other, lambda z: z ^ 4)
    return call(finish_body, (shape(1, GROUP, FF),) * 3, 10, 0, 2 * D * FF)(mine, got)


def local(tokens, expert_ids, gate_values, w_gate, w_up, w_down, cotangent):
    ids, gates = expert_ids.T, gate_values.T
    mm = 2 * ROWS * D * FF
    hbm, vmem = pl.BlockSpec(memory_space=pltpu.HBM), pl.BlockSpec(memory_space=pltpu.VMEM)
    chunks = call(
        place_body,
        shape(EXPERTS, CHUNK, D),
        61,
        4 * mm,
        8 * ROWS * D,
        [
            pltpu.VMEM((EXPERTS, CHUNK, D), BF),
            pltpu.VMEM((2, TOK), jnp.int32),
            pltpu.VMEM((2, TOK), F32),
            pltpu.VMEM((TOK, D), BF),
            pltpu.VMEM((TOK, D), BF),
            pltpu.SemaphoreType.DMA((6,)),
        ],
        in_specs=[hbm] * 4,
        out_specs=hbm,
    )(ids, gates, tokens, cotangent)
    arrived = lax.all_to_all(
        chunks, ("loop", "dp", "tensor"), 0, 0, tiled=True, axis_index_groups=runs()
    )
    kept = shape(ROWS, 2 * D + 3 * FF)
    results, kept = call(
        expert_body,
        (shape(EXPERTS, 2, CHUNK, HALF), kept),
        50,
        6 * mm,
        16 * ROWS * D,
        [
            pltpu.VMEM((EXPERTS, CHUNK, D), BF),
            pltpu.VMEM((EXPERTS, 2, CHUNK, HALF), BF),
            pltpu.VMEM((ROWS, 2 * D + 3 * FF), BF),
            pltpu.VMEM((D, 256), BF),
            pltpu.SemaphoreType.DMA((8,)),
        ],
        in_specs=[hbm, vmem, vmem, vmem],
        out_specs=(hbm, hbm),
    )(arrived, w_gate[0], w_up[0], w_down[0])
    home = lax.all_to_all(
        results.reshape(2 * EXPERTS, CHUNK, HALF), ("loop", "tensor"), 0, 0, tiled=True
    ).reshape(EXPERTS, 2, CHUNK, HALF)
    keep, send = call(
        weights_body,
        (shape(RINGS, GROUP, 3 * FF), shape(RINGS, GROUP, 3 * FF)),
        50,
        3 * mm,
        8 * ROWS * D,
        [
            pltpu.VMEM((ROWS, 2 * D + 3 * FF), BF),
            pltpu.VMEM((DEVS, GROUP, 3 * FF), BF),
            pltpu.SemaphoreType.DMA((4,)),
        ],
        in_specs=[hbm],
    )(kept)
    grads = sum_groups(keep, send)
    mixed, token_grad = call(combine_body, (shape(TOK, HALF), shape(TOK, HALF)), 16, 2 * mm, 8 * ROWS * D)(
        ids, gates, home
    )
    return (mixed, token_grad, *grads)


def solution(mesh):
    spread = P(("loop", "dp"), None)
    weight = P("loop", None, "tensor")
    return jax.shard_map(
        local,
        mesh=mesh,
        in_specs=(spread, spread, spread, weight, weight, weight, spread),
        out_specs=(P(("loop", "dp"), "tensor"),) * 2 + (P("loop", "dp", "tensor"),) * 3,
        check_vma=False,
    )
```

```python
import jax
import jax.numpy as jnp
from jax import lax
from jax.experimental import pallas as pl
from jax.experimental.pallas import tpu as pltpu
from jax.sharding import PartitionSpec as P

BF = jnp.bfloat16
F32 = jnp.float32
TOK = 192
D = 1024
HALF = 512
FF = 384
EXPERTS = 16
MAIN = 32
TAIL = 4
CHUNK = 72
WHOLE = EXPERTS * MAIN
ENDS = EXPERTS * 2 * TAIL
LAST = EXPERTS * TAIL
ROWS = WHOLE + LAST
DEVS = 16
RINGS = 8
GROUP = D // DEVS
MIB = 1024 * 1024


def call(body, outs, vmem, flops=0, nbytes=0, scratch=(), **specs):
    return pl.pallas_call(
        body,
        out_shape=outs,
        **specs,
        scratch_shapes=list(scratch),
        compiler_params=pltpu.CompilerParams(vmem_limit_bytes=int(vmem * MIB)),
        cost_estimate=pl.CostEstimate(flops=flops, bytes_accessed=nbytes, transcendentals=0),
    )


def shape(*dims, dtype=BF):
    return jax.ShapeDtypeStruct(dims, dtype)


def iota(dims, axis):
    return lax.broadcasted_iota(jnp.int32, dims, axis)


def ones_where(condition):
    return jnp.where(condition, 1.0, 0.0).astype(BF)


def dot(a, b):
    return jnp.dot(a, b, preferred_element_type=F32)


def dot_cols(a, b):
    return lax.dot_general(a, b, (((1,), (1,)), ((), ())), preferred_element_type=F32)


def dot_rows(a, b):
    return lax.dot_general(a, b, (((0,), (0,)), ((), ())), preferred_element_type=F32)


def home_places(ids):
    ids = (ids & 3) * 4 + (ids >> 2)
    experts = iota((EXPERTS, TOK), 0)
    named = [experts == ids[k : k + 1, :] for k in range(2)]
    before = ones_where(iota((TOK, TOK), 0) < iota((TOK, TOK), 1))
    count = dot(ones_where(named[0] | named[1]), before)
    return [
        (
            ids[k : k + 1, :],
            jnp.sum(jnp.where(named[k], count, 0.0), axis=0, keepdims=True).astype(jnp.int32),
        )
        for k in range(2)
    ]


def as_column(row):
    diagonal = iota((TOK, TOK), 0) == iota((TOK, TOK), 1)
    return jnp.sum(jnp.where(diagonal, row.astype(F32), 0.0), axis=1, keepdims=True)


def place_body(ids_hbm, gate_hbm, tok_hbm, cot_hbm, out_hbm, out_ref, ids_ref, gate_ref, tok_ref, cot_ref, sems):
    copies = [
        pltpu.make_async_copy(source, target, sems.at[i])
        for i, (source, target) in enumerate(
            ((ids_hbm, ids_ref), (gate_hbm, gate_ref), (cot_hbm, cot_ref), (tok_hbm, tok_ref))
        )
    ]
    for copy in copies:
        copy.start()
    copies[0].wait()
    places = home_places(ids_ref[...])
    tok_rows = [e * CHUNK + jnp.where(p < MAIN, p, p + MAIN) for e, p in places]
    cot_rows = [r + jnp.where(p < MAIN, MAIN, TAIL) for r, (_, p) in zip(tok_rows, places)]
    copies[1].wait()
    gates = [as_column(gate_ref[k : k + 1, :]) for k in range(2)]
    def pick(parts, first, span, stride, rows):
        row = iota((rows, TOK), 0)
        slot = (row & (span - 1)) + (row >> (span.bit_length() - 1)) * stride + first
        hit = slot == parts[0]
        for part in parts[1:]:
            hit |= slot == part
        return ones_where(hit)

    copies[2].wait()
    cot = cot_ref[...].astype(F32)
    weighted = [(gate * cot).astype(BF) for gate in gates]
    copies[3].wait()
    tok = tok_ref[...]
    count = EXPERTS // 2
    for i in range(2):
        block = pl.ds(i * count, count)
        start = i * count * CHUNK
        main = dot(pick(tok_rows, start, MAIN, CHUNK, count * MAIN), tok)
        out_ref[block, :MAIN] = main.astype(BF).reshape(count, MAIN, D)
        main = dot(pick(cot_rows[:1], start + MAIN, MAIN, CHUNK, count * MAIN), weighted[0])
        main += dot(pick(cot_rows[1:], start + MAIN, MAIN, CHUNK, count * MAIN), weighted[1])
        out_ref[block, MAIN : 2 * MAIN] = main.astype(BF).reshape(count, MAIN, D)
        ends = dot(pick(tok_rows, start + 2 * MAIN, 2 * TAIL, CHUNK, count * 2 * TAIL), tok)
        for k in range(2):
            ends += dot(pick(cot_rows[k : k + 1], start + 2 * MAIN, 2 * TAIL, CHUNK, count * 2 * TAIL), weighted[k])
        out_ref[block, 2 * MAIN :] = ends.reshape(count, 2 * TAIL, D).astype(BF)
        copies.append(pltpu.make_async_copy(out_ref.at[block], out_hbm.at[block], sems.at[4 + i]))
        copies[-1].start()
    for copy in copies[4:]:
        copy.wait()


def expert_body(
    in_hbm, gate_ref, up_ref, down_ref, out_hbm, kept_hbm, in_ref, out_ref, kept_ref, rest_ref, sems
):
    quarter = EXPERTS // 4
    quarters = [pl.ds(i * quarter, quarter) for i in range(4)]
    loads = [pltpu.make_async_copy(in_hbm.at[q], in_ref.at[q], sems.at[i]) for i, q in enumerate(quarters)]
    for load in loads:
        load.start()

    def ends_of(axis, skip):
        dims = (ENDS, LAST) if axis == 0 else (LAST, ENDS)
        end, last = iota(dims, axis), iota(dims, 1 - axis)
        return ones_where(end == last + (last >> 2) * TAIL + skip)

    stores = []

    def send(source, target):
        stores.append(pltpu.make_async_copy(source, target, sems.at[4 + len(stores)]))
        stores[-1].start()

    wide = 256
    narrow = FF - wide
    rest_ref[:, :narrow] = gate_ref[:, wide:]
    rest_ref[:, narrow:] = up_ref[:, wide:]
    for i, load in enumerate(loads):
        load.wait()
        part = pl.ds(i * quarter * MAIN, quarter * MAIN)
        kept_ref[part, :D] = in_ref[quarters[i], :MAIN, :].reshape(quarter * MAIN, D)
        kept_ref[part, D : 2 * D] = in_ref[quarters[i], MAIN : 2 * MAIN, :].reshape(quarter * MAIN, D)
    tail = in_ref[:, 2 * MAIN :, :].astype(F32).reshape(ENDS, D).astype(BF)
    kept_ref[WHOLE:, :D] = dot(ends_of(1, 0), tail).astype(BF)
    kept_ref[WHOLE:, D : 2 * D] = dot(ends_of(1, TAIL), tail).astype(BF)
    send(kept_ref.at[:, : 2 * D], kept_hbm.at[:, : 2 * D])
    rows = kept_ref[:, :D]
    rest = dot(rows, rest_ref[...])
    gate_pre = jnp.concatenate([dot(rows, gate_ref[:, :wide]), rest[:, :narrow]], axis=1)
    up_pre = jnp.concatenate([dot(rows, up_ref[:, :wide]), rest[:, narrow:]], axis=1)
    hidden_grad = dot(kept_ref[:, D : 2 * D], down_ref[...])
    sigma = jax.nn.sigmoid(gate_pre)
    silu = gate_pre * sigma
    gate_grad = (hidden_grad * up_pre * (sigma * (1.0 + gate_pre * (1.0 - sigma)))).astype(BF)
    up_grad = (hidden_grad * silu).astype(BF)
    hidden = (silu * up_pre).astype(BF)
    for i, value in enumerate((gate_grad, up_grad, hidden)):
        kept_ref[:, 2 * D + i * FF : 2 * D + (i + 1) * FF] = value
    send(kept_ref.at[:, 2 * D :], kept_hbm.at[:, 2 * D :])
    rest = jnp.concatenate([gate_grad[:, wide:], up_grad[:, wide:]], axis=1)
    for h in range(2):
        part = pl.ds(h * HALF, HALF)
        output = dot_cols(hidden, down_ref[part, :])
        input_grad = dot_cols(gate_grad[:, :wide], gate_ref[part, :wide])
        input_grad += dot_cols(up_grad[:, :wide], up_ref[part, :wide])
        input_grad = (input_grad + dot_cols(rest, rest_ref[part, :])).astype(BF)
        output = output.astype(BF)
        ends = dot(ends_of(0, 0), output[WHOLE:]) + dot(ends_of(0, TAIL), input_grad[WHOLE:])
        out_ref[:, h, :MAIN, :] = output[:WHOLE].reshape(EXPERTS, MAIN, HALF)
        out_ref[:, h, MAIN : 2 * MAIN, :] = input_grad[:WHOLE].reshape(EXPERTS, MAIN, HALF)
        out_ref[:, h, 2 * MAIN :, :] = ends.reshape(EXPERTS, 2 * TAIL, HALF).astype(BF)
        send(out_ref.at[:, h], out_hbm.at[:, h])
    for store in stores:
        store.wait()


def weights_body(kept_hbm, keep_ref, send_ref, kept_ref, all_ref, sems):
    core = lax.axis_index("dp") & 1
    rows, grads = pl.ds(0, D), pl.ds(2 * D, 2 * FF)
    back, hidden = pl.ds(D, D), pl.ds(2 * D + 2 * FF, FF)
    copies = [
        pltpu.make_async_copy(kept_hbm.at[:, part], kept_ref.at[:, part], sems.at[i])
        for i, part in enumerate((rows, grads, back, hidden))
    ]
    for copy in copies:
        copy.start()
    for copy in copies[:2]:
        copy.wait()
    both = dot_rows(kept_ref[:, rows], kept_ref[:, grads]).astype(BF)
    all_ref[:, :, : 2 * FF] = both.reshape(DEVS, GROUP, 2 * FF)
    for copy in copies[2:]:
        copy.wait()
    down = dot_rows(kept_ref[:, back], kept_ref[:, hidden]).astype(BF)
    all_ref[:, :, 2 * FF :] = down.reshape(DEVS, GROUP, FF)
    for i in range(RINGS):
        keep_ref[i] = all_ref[2 * i + core]
        send_ref[i] = all_ref[2 * i + 1 - core]


def around(z):
    return (z + 2 * (z & 1) - 1) & (RINGS - 1)


def add(left, right):
    return (left.astype(F32) + right.astype(F32)).astype(BF)


def split_body(keep_ref, got_ref, *outs):
    z = lax.axis_index("dp") >> 1
    half = GROUP // 2
    for part, (own, partner, later) in enumerate(((z, around(z), lambda i: i ^ 1), (z, z ^ 1, around))):
        rows = pl.ds(part * half, half)
        for ref, chip in zip(outs[2 * part : 2 * part + 2], (own, partner)):
            for i, chunk in enumerate((chip, chip ^ 4, later(chip), later(chip) ^ 4)):
                ref[i] = add(keep_ref[chunk, rows], got_ref[chunk, rows])


def halve_body(*refs):
    for mine_ref, got_ref, keep_ref, send_ref in (refs[0::2], refs[1::2]):
        half = mine_ref.shape[0] // 2
        keep_ref[...] = add(mine_ref[:half], got_ref[:half])
        send_ref[...] = add(mine_ref[half:], got_ref[half:])


def join_body(mine0_ref, mine1_ref, got0_ref, got1_ref, keep_ref, send_ref):
    half = GROUP // 2
    for part, (mine_ref, got_ref) in enumerate(((mine0_ref, got0_ref), (mine1_ref, got1_ref))):
        rows = pl.ds(part * half, half)
        keep_ref[0, rows] = add(mine_ref[0], got_ref[0])
        send_ref[0, rows] = add(mine_ref[1], got_ref[1])


def finish_body(own_ref, got_ref, gate_ref, up_ref, down_ref):
    total = add(own_ref[...], got_ref[...])
    gate_ref[...] = total[:, :, :FF]
    up_ref[...] = total[:, :, FF : 2 * FF]
    down_ref[...] = total[:, :, 2 * FF :]


def combine_body(ids_ref, gate_ref, back_ref, mixed_ref, grad_ref):
    places = home_places(ids_ref[...])
    gates = gate_ref[...]
    main_column = iota((TOK, WHOLE), 1).astype(F32)
    tail_column = iota((TOK, ENDS), 1).astype(F32)
    main = [jnp.zeros((TOK, WHOLE), F32)] * 2
    tail = [jnp.zeros((TOK, ENDS), F32)] * 2
    for k, (expert, place) in enumerate(places):
        gate = as_column(gates[k : k + 1, :])
        in_main = main_column == as_column(jnp.where(place < MAIN, expert * MAIN + place, -1))
        at = as_column(jnp.where(place < MAIN, -8, expert * 2 * TAIL + place - MAIN))
        main = [jnp.where(in_main, gate, main[0]), jnp.where(in_main, 1.0, main[1])]
        tail = [jnp.where(tail_column == at, gate, tail[0]), jnp.where(tail_column == at + TAIL, 1.0, tail[1])]

    def split(mix):
        high = mix.astype(BF)
        return high, (mix - high.astype(F32)).astype(BF)

    outs = [jnp.zeros((TOK, HALF), F32)] * 2
    for h in range(2):
        ends = back_ref[:, h, 2 * MAIN :, :].astype(F32).reshape(ENDS, HALF).astype(BF)
        output = back_ref[:, h, :MAIN, :].reshape(WHOLE, HALF)
        input_grad = back_ref[:, h, MAIN : 2 * MAIN, :].reshape(WHOLE, HALF)
        for part, rows in ((main, output), (tail, ends)):
            for piece in split(part[0]):
                outs[0] = outs[0] + dot(piece, rows)
        outs[1] = outs[1] + dot(main[1].astype(BF), input_grad) + dot(tail[1].astype(BF), ends)
    mixed_ref[...] = outs[0].astype(BF)
    grad_ref[...] = outs[1].astype(BF)


def runs():
    out, home = [], []
    device = lambda y, x, dp, high: ((4 * y + x) * DEVS + dp) * 2 + high
    for dp in range(DEVS):
        for start in (2 * (dp % 2), 2 * (dp % 2) + 4):
            high = {(start + i) % 4: (start + i) % 8 // 4 for i in range(4)}
            out.append([device(y, x, dp, high[y]) for x in range(4) for y in range(4)])
        home.append([device(y, x, dp, high) for x in range(4) for y in range(4) for high in range(2)])
    return out, home


def along_z(value, target):
    return lax.ppermute(value, "dp", [(2 * z + core, 2 * (target(z) % RINGS) + core) for z in range(RINGS) for core in range(2)])


def sum_groups(keep, send):
    some = lambda count: shape(count, GROUP // 2, 3 * FF)
    whole = shape(1, GROUP, 3 * FF)
    got = lax.ppermute(send, "dp", [(i, i ^ 1) for i in range(DEVS)])
    mine0, other0, mine1, other1 = call(split_body, (some(4),) * 4, 10, 0, 12 * D * FF)(keep, got)
    got0, got1 = along_z(other0, around), along_z(other1, lambda z: z ^ 1)
    mine0, mine1, other0, other1 = call(halve_body, (some(2),) * 4, 10, 0, 6 * D * FF)(mine0, mine1, got0, got1)
    got0, got1 = along_z(other0, lambda z: z ^ 1), along_z(other1, around)
    mine, other = call(join_body, (whole, whole), 10, 0, 3 * D * FF)(mine0, mine1, got0, got1)
    got = along_z(other, lambda z: z ^ 4)
    return call(finish_body, (shape(1, GROUP, FF),) * 3, 10, 0, 2 * D * FF)(mine, got)


def local(tokens, expert_ids, gate_values, w_gate, w_up, w_down, cotangent):
    ids, gates = expert_ids.T, gate_values.T
    mm = 2 * ROWS * D * FF
    hbm, vmem = pl.BlockSpec(memory_space=pltpu.HBM), pl.BlockSpec(memory_space=pltpu.VMEM)
    chunks = call(
        place_body,
        shape(EXPERTS, CHUNK, D),
        61,
        4 * mm,
        8 * ROWS * D,
        [
            pltpu.VMEM((EXPERTS, CHUNK, D), BF),
            pltpu.VMEM((2, TOK), jnp.int32),
            pltpu.VMEM((2, TOK), F32),
            pltpu.VMEM((TOK, D), BF),
            pltpu.VMEM((TOK, D), BF),
            pltpu.SemaphoreType.DMA((6,)),
        ],
        in_specs=[hbm] * 4,
        out_specs=hbm,
    )(ids, gates, tokens, cotangent)
    everywhere = ("loop", "dp", "tensor")
    out_groups, home_groups = runs()
    arrived = lax.all_to_all(chunks, everywhere, 0, 0, tiled=True, axis_index_groups=out_groups)
    kept = shape(ROWS, 2 * D + 3 * FF)
    results, kept = call(
        expert_body,
        (shape(EXPERTS, 2, CHUNK, HALF), kept),
        50,
        6 * mm,
        16 * ROWS * D,
        [
            pltpu.VMEM((EXPERTS, CHUNK, D), BF),
            pltpu.VMEM((EXPERTS, 2, CHUNK, HALF), BF),
            pltpu.VMEM((ROWS, 2 * D + 3 * FF), BF),
            pltpu.VMEM((D, 256), BF),
            pltpu.SemaphoreType.DMA((8,)),
        ],
        in_specs=[hbm, vmem, vmem, vmem],
        out_specs=(hbm, hbm),
    )(arrived, w_gate[0], w_up[0], w_down[0])
    home = lax.all_to_all(
        results.reshape(2 * EXPERTS, CHUNK, HALF), everywhere, 0, 0, tiled=True, axis_index_groups=home_groups
    ).reshape(EXPERTS, 2, CHUNK, HALF)
    keep, send = call(
        weights_body,
        (shape(RINGS, GROUP, 3 * FF), shape(RINGS, GROUP, 3 * FF)),
        50,
        3 * mm,
        8 * ROWS * D,
        [
            pltpu.VMEM((ROWS, 2 * D + 3 * FF), BF),
            pltpu.VMEM((DEVS, GROUP, 3 * FF), BF),
            pltpu.SemaphoreType.DMA((4,)),
        ],
        in_specs=[hbm],
    )(kept)
    grads = sum_groups(keep, send)
    mixed, token_grad = call(combine_body, (shape(TOK, HALF), shape(TOK, HALF)), 16, 2 * mm, 8 * ROWS * D)(
        ids, gates, home
    )
    return (mixed, token_grad, *grads)


def solution(mesh):
    spread = P(("loop", "dp"), None)
    weight = P("loop", None, "tensor")
    return jax.shard_map(
        local,
        mesh=mesh,
        in_specs=(spread, spread, spread, weight, weight, weight, spread),
        out_specs=(P(("loop", "dp"), "tensor"),) * 2 + (P("loop", "dp", "tensor"),) * 3,
        check_vma=False,
    )
```

```python
import jax
import jax.numpy as jnp
from jax import lax
from jax.experimental import pallas as pl
from jax.experimental.pallas import tpu as pltpu
from jax.sharding import PartitionSpec as P

BF = jnp.bfloat16
F32 = jnp.float32
TOK = 192
D = 1024
HALF = 512
FF = 384
EXPERTS = 16
MAIN = 32
TAIL = 4
CHUNK = 72
WHOLE = EXPERTS * MAIN
ENDS = EXPERTS * 2 * TAIL
LAST = EXPERTS * TAIL
ROWS = WHOLE + LAST
DEVS = 16
RINGS = 8
GROUP = D // DEVS
MIB = 1024 * 1024


def call(body, outs, vmem, flops=0, nbytes=0, scratch=(), **specs):
    return pl.pallas_call(
        body,
        out_shape=outs,
        **specs,
        scratch_shapes=list(scratch),
        compiler_params=pltpu.CompilerParams(vmem_limit_bytes=int(vmem * MIB)),
        cost_estimate=pl.CostEstimate(flops=flops, bytes_accessed=nbytes, transcendentals=0),
    )


def shape(*dims, dtype=BF):
    return jax.ShapeDtypeStruct(dims, dtype)


def iota(dims, axis):
    return lax.broadcasted_iota(jnp.int32, dims, axis)


def ones_where(condition):
    return jnp.where(condition, 1.0, 0.0).astype(BF)


def dot(a, b):
    return jnp.dot(a, b, preferred_element_type=F32)


def dot_cols(a, b):
    return lax.dot_general(a, b, (((1,), (1,)), ((), ())), preferred_element_type=F32)


def dot_rows(a, b):
    return lax.dot_general(a, b, (((0,), (0,)), ((), ())), preferred_element_type=F32)


def home_places(ids):
    ids = (ids & 3) * 4 + (ids >> 2)
    experts = iota((EXPERTS, TOK), 0)
    named = [experts == ids[k : k + 1, :] for k in range(2)]
    before = ones_where(iota((TOK, TOK), 0) < iota((TOK, TOK), 1))
    count = dot(ones_where(named[0] | named[1]), before)
    return [
        (
            ids[k : k + 1, :],
            jnp.sum(jnp.where(named[k], count, 0.0), axis=0, keepdims=True).astype(jnp.int32),
        )
        for k in range(2)
    ]


def as_column(row):
    diagonal = iota((TOK, TOK), 0) == iota((TOK, TOK), 1)
    return jnp.sum(jnp.where(diagonal, row.astype(F32), 0.0), axis=1, keepdims=True)


def place_body(ids_hbm, gate_hbm, tok_hbm, cot_hbm, out_hbm, out_ref, ids_ref, gate_ref, tok_ref, cot_ref, sems):
    copies = [
        pltpu.make_async_copy(source, target, sems.at[i])
        for i, (source, target) in enumerate(
            ((ids_hbm, ids_ref), (gate_hbm, gate_ref), (cot_hbm, cot_ref), (tok_hbm, tok_ref))
        )
    ]
    for copy in copies:
        copy.start()
    copies[0].wait()
    places = home_places(ids_ref[...])
    tok_rows = [e * CHUNK + jnp.where(p < MAIN, p, p + MAIN) for e, p in places]
    cot_rows = [r + jnp.where(p < MAIN, MAIN, TAIL) for r, (_, p) in zip(tok_rows, places)]
    copies[1].wait()
    gates = [as_column(gate_ref[k : k + 1, :]) for k in range(2)]
    def pick(parts, first, span, stride, rows):
        row = iota((rows, TOK), 0)
        slot = (row & (span - 1)) + (row >> (span.bit_length() - 1)) * stride + first
        hit = slot == parts[0]
        for part in parts[1:]:
            hit |= slot == part
        return ones_where(hit)

    copies[2].wait()
    cot = cot_ref[...].astype(F32)
    weighted = [(gate * cot).astype(BF) for gate in gates]
    copies[3].wait()
    tok = tok_ref[...]
    count = EXPERTS // 2
    for i in range(2):
        block = pl.ds(i * count, count)
        start = i * count * CHUNK
        main = dot(pick(tok_rows, start, MAIN, CHUNK, count * MAIN), tok)
        out_ref[block, :MAIN] = main.astype(BF).reshape(count, MAIN, D)
        main = dot(pick(cot_rows[:1], start + MAIN, MAIN, CHUNK, count * MAIN), weighted[0])
        main += dot(pick(cot_rows[1:], start + MAIN, MAIN, CHUNK, count * MAIN), weighted[1])
        out_ref[block, MAIN : 2 * MAIN] = main.astype(BF).reshape(count, MAIN, D)
        ends = dot(pick(tok_rows, start + 2 * MAIN, 2 * TAIL, CHUNK, count * 2 * TAIL), tok)
        for k in range(2):
            ends += dot(pick(cot_rows[k : k + 1], start + 2 * MAIN, 2 * TAIL, CHUNK, count * 2 * TAIL), weighted[k])
        out_ref[block, 2 * MAIN :] = ends.reshape(count, 2 * TAIL, D).astype(BF)
        copies.append(pltpu.make_async_copy(out_ref.at[block], out_hbm.at[block], sems.at[4 + i]))
        copies[-1].start()
    for copy in copies[4:]:
        copy.wait()


def expert_body(
    in_hbm, gate_ref, up_ref, down_ref, out_hbm, kept_hbm, in_ref, out_ref, kept_ref, rest_ref, sems
):
    quarter = EXPERTS // 4
    quarters = [pl.ds(i * quarter, quarter) for i in range(4)]
    loads = [pltpu.make_async_copy(in_hbm.at[q], in_ref.at[q], sems.at[i]) for i, q in enumerate(quarters)]
    for load in loads:
        load.start()

    def ends_of(axis, skip):
        dims = (ENDS, LAST) if axis == 0 else (LAST, ENDS)
        end, last = iota(dims, axis), iota(dims, 1 - axis)
        return ones_where(end == last + (last >> 2) * TAIL + skip)

    stores = []

    def send(source, target):
        stores.append(pltpu.make_async_copy(source, target, sems.at[4 + len(stores)]))
        stores[-1].start()

    wide = 256
    narrow = FF - wide
    rest_ref[:, :narrow] = gate_ref[:, wide:]
    rest_ref[:, narrow:] = up_ref[:, wide:]
    for i, load in enumerate(loads):
        load.wait()
        part = pl.ds(i * quarter * MAIN, quarter * MAIN)
        kept_ref[part, :D] = in_ref[quarters[i], :MAIN, :].reshape(quarter * MAIN, D)
        kept_ref[part, D : 2 * D] = in_ref[quarters[i], MAIN : 2 * MAIN, :].reshape(quarter * MAIN, D)
    tail = in_ref[:, 2 * MAIN :, :].astype(F32).reshape(ENDS, D).astype(BF)
    kept_ref[WHOLE:, :D] = dot(ends_of(1, 0), tail).astype(BF)
    kept_ref[WHOLE:, D : 2 * D] = dot(ends_of(1, TAIL), tail).astype(BF)
    send(kept_ref.at[:, : 2 * D], kept_hbm.at[:, : 2 * D])
    rows = kept_ref[:, :D]
    rest = dot(rows, rest_ref[...])
    gate_pre = jnp.concatenate([dot(rows, gate_ref[:, :wide]), rest[:, :narrow]], axis=1)
    up_pre = jnp.concatenate([dot(rows, up_ref[:, :wide]), rest[:, narrow:]], axis=1)
    hidden_grad = dot(kept_ref[:, D : 2 * D], down_ref[...])
    sigma = jax.nn.sigmoid(gate_pre)
    silu = gate_pre * sigma
    gate_grad = (hidden_grad * up_pre * (sigma * (1.0 + gate_pre * (1.0 - sigma)))).astype(BF)
    up_grad = (hidden_grad * silu).astype(BF)
    hidden = (silu * up_pre).astype(BF)
    for i, value in enumerate((gate_grad, up_grad, hidden)):
        kept_ref[:, 2 * D + i * FF : 2 * D + (i + 1) * FF] = value
    send(kept_ref.at[:, 2 * D :], kept_hbm.at[:, 2 * D :])
    rest = jnp.concatenate([gate_grad[:, wide:], up_grad[:, wide:]], axis=1)
    for h in range(2):
        part = pl.ds(h * HALF, HALF)
        output = dot_cols(hidden, down_ref[part, :])
        input_grad = dot_cols(gate_grad[:, :wide], gate_ref[part, :wide])
        input_grad += dot_cols(up_grad[:, :wide], up_ref[part, :wide])
        input_grad = (input_grad + dot_cols(rest, rest_ref[part, :])).astype(BF)
        output = output.astype(BF)
        ends = dot(ends_of(0, 0), output[WHOLE:]) + dot(ends_of(0, TAIL), input_grad[WHOLE:])
        out_ref[h, :, :MAIN, :] = output[:WHOLE].reshape(EXPERTS, MAIN, HALF)
        out_ref[h, :, MAIN : 2 * MAIN, :] = input_grad[:WHOLE].reshape(EXPERTS, MAIN, HALF)
        out_ref[h, :, 2 * MAIN :, :] = ends.reshape(EXPERTS, 2 * TAIL, HALF).astype(BF)
        send(out_ref.at[h], out_hbm.at[h])
    for store in stores:
        store.wait()


def weights_body(kept_hbm, keep_ref, send_ref, kept_ref, all_ref, sems):
    core = lax.axis_index("dp") & 1
    rows, grads = pl.ds(0, D), pl.ds(2 * D, 2 * FF)
    back, hidden = pl.ds(D, D), pl.ds(2 * D + 2 * FF, FF)
    copies = [
        pltpu.make_async_copy(kept_hbm.at[:, part], kept_ref.at[:, part], sems.at[i])
        for i, part in enumerate((rows, grads, back, hidden))
    ]
    for copy in copies:
        copy.start()
    for copy in copies[:2]:
        copy.wait()
    both = dot_rows(kept_ref[:, rows], kept_ref[:, grads]).astype(BF)
    all_ref[:, :, : 2 * FF] = both.reshape(DEVS, GROUP, 2 * FF)
    for copy in copies[2:]:
        copy.wait()
    down = dot_rows(kept_ref[:, back], kept_ref[:, hidden]).astype(BF)
    all_ref[:, :, 2 * FF :] = down.reshape(DEVS, GROUP, FF)
    for i in range(RINGS):
        keep_ref[i] = all_ref[2 * i + core]
        send_ref[i] = all_ref[2 * i + 1 - core]


def around(z):
    return (z + 2 * (z & 1) - 1) & (RINGS - 1)


def add(left, right):
    return (left.astype(F32) + right.astype(F32)).astype(BF)


def split_body(keep_ref, got_ref, *outs):
    z = lax.axis_index("dp") >> 1
    half = GROUP // 2
    for part, (own, partner, later) in enumerate(((z, z ^ 1, around), (z, around(z), lambda i: i ^ 1))):
        rows = pl.ds(part * half, half)
        for ref, chip in zip(outs[2 * part : 2 * part + 2], (own, partner)):
            for i, chunk in enumerate((chip, chip ^ 4, later(chip), later(chip) ^ 4)):
                ref[i] = add(keep_ref[chunk, rows], got_ref[chunk, rows])


def halve_body(*refs):
    for mine_ref, got_ref, keep_ref, send_ref in (refs[0::2], refs[1::2]):
        half = mine_ref.shape[0] // 2
        keep_ref[...] = add(mine_ref[:half], got_ref[:half])
        send_ref[...] = add(mine_ref[half:], got_ref[half:])


def join_body(got1_ref, got0_ref, mine1_ref, mine0_ref, keep_ref, send_ref):
    half = GROUP // 2
    for part, (mine_ref, got_ref) in enumerate(((mine0_ref, got0_ref), (mine1_ref, got1_ref))):
        rows = pl.ds(part * half, half)
        keep_ref[0, rows] = add(mine_ref[0], got_ref[0])
        send_ref[0, rows] = add(mine_ref[1], got_ref[1])


def finish_body(own_ref, got_ref, gate_ref, up_ref, down_ref):
    total = add(own_ref[...], got_ref[...])
    gate_ref[...] = total[:, :, :FF]
    up_ref[...] = total[:, :, FF : 2 * FF]
    down_ref[...] = total[:, :, 2 * FF :]


def combine_body(ids_ref, gate_ref, back_ref, mixed_ref, grad_ref):
    places = home_places(ids_ref[...])
    gates = gate_ref[...]
    main_column = iota((TOK, WHOLE), 1).astype(F32)
    tail_column = iota((TOK, ENDS), 1).astype(F32)
    main = [jnp.zeros((TOK, WHOLE), F32)] * 2
    tail = [jnp.zeros((TOK, ENDS), F32)] * 2
    for k, (expert, place) in enumerate(places):
        gate = as_column(gates[k : k + 1, :])
        in_main = main_column == as_column(jnp.where(place < MAIN, expert * MAIN + place, -1))
        at = as_column(jnp.where(place < MAIN, -8, expert * 2 * TAIL + place - MAIN))
        main = [jnp.where(in_main, gate, main[0]), jnp.where(in_main, 1.0, main[1])]
        tail = [jnp.where(tail_column == at, gate, tail[0]), jnp.where(tail_column == at + TAIL, 1.0, tail[1])]

    def split(mix):
        high = mix.astype(BF)
        return high, (mix - high.astype(F32)).astype(BF)

    outs = [jnp.zeros((TOK, HALF), F32)] * 2
    for h in range(2):
        ends = back_ref[h, :, 2 * MAIN :, :].astype(F32).reshape(ENDS, HALF).astype(BF)
        output = back_ref[h, :, :MAIN, :].reshape(WHOLE, HALF)
        input_grad = back_ref[h, :, MAIN : 2 * MAIN, :].reshape(WHOLE, HALF)
        for part, rows in ((main, output), (tail, ends)):
            for piece in split(part[0]):
                outs[0] = outs[0] + dot(piece, rows)
        outs[1] = outs[1] + dot(main[1].astype(BF), input_grad) + dot(tail[1].astype(BF), ends)
    mixed_ref[...] = outs[0].astype(BF)
    grad_ref[...] = outs[1].astype(BF)


def runs():
    out, home = [], []
    device = lambda y, x, dp, high: ((4 * y + x) * DEVS + dp) * 2 + high
    for dp in range(DEVS):
        for start in (2 * (dp % 2), 2 * (dp % 2) + 4):
            high = {(start + i) % 4: (start + i) % 8 // 4 for i in range(4)}
            out.append([device(y, x, dp, high[y]) for x in range(4) for y in range(4)])
        home.append([device(y, x, dp, high) for high in range(2) for x in range(4) for y in range(4)])
    return out, home


def along_z(value, target):
    return lax.ppermute(value, "dp", [(2 * z + core, 2 * (target(z) % RINGS) + core) for z in range(RINGS) for core in range(2)])


def sum_groups(keep, send):
    some = lambda count: shape(count, GROUP // 2, 3 * FF)
    whole = shape(1, GROUP, 3 * FF)
    got = lax.ppermute(send, "dp", [(i, i ^ 1) for i in range(DEVS)])
    mine0, other0, mine1, other1 = call(split_body, (some(4),) * 4, 10, 0, 12 * D * FF)(keep, got)
    got0, got1 = along_z(other0, lambda z: z ^ 1), along_z(other1, around)
    mine0, mine1, other0, other1 = call(halve_body, (some(2),) * 4, 10, 0, 6 * D * FF)(mine0, mine1, got0, got1)
    got1, got0 = along_z(other1, lambda z: z ^ 1), along_z(other0, around)
    mine, other = call(join_body, (whole, whole), 10, 0, 3 * D * FF)(got1, got0, mine1, mine0)
    got = along_z(other, lambda z: z ^ 4)
    return call(finish_body, (shape(1, GROUP, FF),) * 3, 10, 0, 2 * D * FF)(mine, got)


def local(tokens, expert_ids, gate_values, w_gate, w_up, w_down, cotangent):
    ids, gates = expert_ids.T, gate_values.T
    mm = 2 * ROWS * D * FF
    hbm, vmem = pl.BlockSpec(memory_space=pltpu.HBM), pl.BlockSpec(memory_space=pltpu.VMEM)
    chunks = call(
        place_body,
        shape(EXPERTS, CHUNK, D),
        61,
        4 * mm,
        8 * ROWS * D,
        [
            pltpu.VMEM((EXPERTS, CHUNK, D), BF),
            pltpu.VMEM((2, TOK), jnp.int32),
            pltpu.VMEM((2, TOK), F32),
            pltpu.VMEM((TOK, D), BF),
            pltpu.VMEM((TOK, D), BF),
            pltpu.SemaphoreType.DMA((6,)),
        ],
        in_specs=[hbm] * 4,
        out_specs=hbm,
    )(ids, gates, tokens, cotangent)
    everywhere = ("loop", "dp", "tensor")
    out_groups, home_groups = runs()
    arrived = lax.all_to_all(chunks, everywhere, 0, 0, tiled=True, axis_index_groups=out_groups)
    kept = shape(ROWS, 2 * D + 3 * FF)
    results, kept = call(
        expert_body,
        (shape(2, EXPERTS, CHUNK, HALF), kept),
        50,
        6 * mm,
        16 * ROWS * D,
        [
            pltpu.VMEM((EXPERTS, CHUNK, D), BF),
            pltpu.VMEM((2, EXPERTS, CHUNK, HALF), BF),
            pltpu.VMEM((ROWS, 2 * D + 3 * FF), BF),
            pltpu.VMEM((D, 256), BF),
            pltpu.SemaphoreType.DMA((8,)),
        ],
        in_specs=[hbm, vmem, vmem, vmem],
        out_specs=(hbm, hbm),
    )(arrived, w_gate[0], w_up[0], w_down[0])
    home = lax.all_to_all(
        results.reshape(2 * EXPERTS, CHUNK, HALF), everywhere, 0, 0, tiled=True, axis_index_groups=home_groups
    ).reshape(2, EXPERTS, CHUNK, HALF)
    keep, send = call(
        weights_body,
        (shape(RINGS, GROUP, 3 * FF), shape(RINGS, GROUP, 3 * FF)),
        50,
        3 * mm,
        8 * ROWS * D,
        [
            pltpu.VMEM((ROWS, 2 * D + 3 * FF), BF),
            pltpu.VMEM((DEVS, GROUP, 3 * FF), BF),
            pltpu.SemaphoreType.DMA((4,)),
        ],
        in_specs=[hbm],
    )(kept)
    grads = sum_groups(keep, send)
    mixed, token_grad = call(combine_body, (shape(TOK, HALF), shape(TOK, HALF)), 16, 2 * mm, 8 * ROWS * D)(
        ids, gates, home
    )
    return (mixed, token_grad, *grads)


def solution(mesh):
    spread = P(("loop", "dp"), None)
    weight = P("loop", None, "tensor")
    return jax.shard_map(
        local,
        mesh=mesh,
        in_specs=(spread, spread, spread, weight, weight, weight, spread),
        out_specs=(P(("loop", "dp"), "tensor"),) * 2 + (P("loop", "dp", "tensor"),) * 3,
        check_vma=False,
    )
```

```python
import jax
import jax.numpy as jnp
from jax import lax
from jax.experimental import pallas as pl
from jax.experimental.pallas import tpu as pltpu
from jax.sharding import PartitionSpec as P

BF = jnp.bfloat16
F32 = jnp.float32
TOK = 192
D = 1024
HALF = 512
FF = 384
EXPERTS = 16
MAIN = 32
TAIL = 4
CHUNK = 72
WHOLE = EXPERTS * MAIN
ENDS = EXPERTS * 2 * TAIL
LAST = EXPERTS * TAIL
ROWS = WHOLE + LAST
DEVS = 16
RINGS = 8
GROUP = D // DEVS
MIB = 1024 * 1024


def call(body, outs, vmem, flops=0, nbytes=0, scratch=(), **specs):
    return pl.pallas_call(
        body,
        out_shape=outs,
        **specs,
        scratch_shapes=list(scratch),
        compiler_params=pltpu.CompilerParams(vmem_limit_bytes=int(vmem * MIB)),
        cost_estimate=pl.CostEstimate(flops=flops, bytes_accessed=nbytes, transcendentals=0),
    )


def shape(*dims, dtype=BF):
    return jax.ShapeDtypeStruct(dims, dtype)


def iota(dims, axis):
    return lax.broadcasted_iota(jnp.int32, dims, axis)


def ones_where(condition):
    return jnp.where(condition, 1.0, 0.0).astype(BF)


def dot(a, b):
    return jnp.dot(a, b, preferred_element_type=F32)


def dot_cols(a, b):
    return lax.dot_general(a, b, (((1,), (1,)), ((), ())), preferred_element_type=F32)


def dot_rows(a, b):
    return lax.dot_general(a, b, (((0,), (0,)), ((), ())), preferred_element_type=F32)


def home_places(ids):
    ids = (ids & 3) * 4 + (ids >> 2)
    experts = iota((EXPERTS, TOK), 0)
    named = [experts == ids[k : k + 1, :] for k in range(2)]
    before = ones_where(iota((TOK, TOK), 0) < iota((TOK, TOK), 1))
    count = dot(ones_where(named[0] | named[1]), before)
    return [
        (
            ids[k : k + 1, :],
            jnp.sum(jnp.where(named[k], count, 0.0), axis=0, keepdims=True).astype(jnp.int32),
        )
        for k in range(2)
    ]


def as_column(row):
    diagonal = iota((TOK, TOK), 0) == iota((TOK, TOK), 1)
    return jnp.sum(jnp.where(diagonal, row.astype(F32), 0.0), axis=1, keepdims=True)


def place_body(ids_hbm, gate_hbm, tok_hbm, cot_hbm, out_hbm, out_ref, ids_ref, gate_ref, tok_ref, cot_ref, sems):
    copies = [
        pltpu.make_async_copy(source, target, sems.at[i])
        for i, (source, target) in enumerate(
            ((ids_hbm, ids_ref), (gate_hbm, gate_ref), (tok_hbm, tok_ref), (cot_hbm, cot_ref))
        )
    ]
    for copy in copies:
        copy.start()
    copies[0].wait()
    places = home_places(ids_ref[...])
    tok_rows = [e * CHUNK + jnp.where(p < MAIN, p, p + MAIN) for e, p in places]
    cot_rows = [r + jnp.where(p < MAIN, MAIN, TAIL) for r, (_, p) in zip(tok_rows, places)]
    copies[1].wait()
    gates = [as_column(gate_ref[k : k + 1, :]) for k in range(2)]
    def pick(parts, first, span, stride, rows):
        row = iota((rows, TOK), 0)
        slot = (row & (span - 1)) + (row >> (span.bit_length() - 1)) * stride + first
        hit = slot == parts[0]
        for part in parts[1:]:
            hit |= slot == part
        return ones_where(hit)

    copies[2].wait()
    tok = tok_ref[...]
    count = EXPERTS // 2
    for i in range(2):
        main = dot(pick(tok_rows, i * count * CHUNK, MAIN, CHUNK, count * MAIN), tok)
        out_ref[i * count : (i + 1) * count, :MAIN] = main.astype(BF).reshape(count, MAIN, D)
    copies[3].wait()
    cot = cot_ref[...].astype(F32)
    weighted = [(gate * cot).astype(BF) for gate in gates]
    for i in range(2):
        block = pl.ds(i * count, count)
        start = i * count * CHUNK
        main = dot(pick(cot_rows[:1], start + MAIN, MAIN, CHUNK, count * MAIN), weighted[0])
        main += dot(pick(cot_rows[1:], start + MAIN, MAIN, CHUNK, count * MAIN), weighted[1])
        out_ref[block, MAIN : 2 * MAIN] = main.astype(BF).reshape(count, MAIN, D)
        ends = dot(pick(tok_rows, start + 2 * MAIN, 2 * TAIL, CHUNK, count * 2 * TAIL), tok)
        for k in range(2):
            ends += dot(pick(cot_rows[k : k + 1], start + 2 * MAIN, 2 * TAIL, CHUNK, count * 2 * TAIL), weighted[k])
        out_ref[block, 2 * MAIN :] = ends.reshape(count, 2 * TAIL, D).astype(BF)
        copies.append(pltpu.make_async_copy(out_ref.at[block], out_hbm.at[block], sems.at[4 + i]))
        copies[-1].start()
    for copy in copies[4:]:
        copy.wait()


def expert_body(
    in_hbm, gate_ref, up_ref, down_ref, out_hbm, kept_hbm, in_ref, out_ref, kept_ref, rest_ref, sems
):
    quarter = EXPERTS // 4
    quarters = [pl.ds(i * quarter, quarter) for i in range(4)]
    loads = [pltpu.make_async_copy(in_hbm.at[q], in_ref.at[q], sems.at[i]) for i, q in enumerate(quarters)]
    for load in loads:
        load.start()

    def ends_of(axis, skip):
        dims = (ENDS, LAST) if axis == 0 else (LAST, ENDS)
        end, last = iota(dims, axis), iota(dims, 1 - axis)
        return ones_where(end == last + (last >> 2) * TAIL + skip)

    stores = []

    def send(source, target):
        stores.append(pltpu.make_async_copy(source, target, sems.at[4 + len(stores)]))
        stores[-1].start()

    wide = 256
    narrow = FF - wide
    rest_ref[:, :narrow] = gate_ref[:, wide:]
    rest_ref[:, narrow:] = up_ref[:, wide:]
    for i, load in enumerate(loads):
        load.wait()
        part = pl.ds(i * quarter * MAIN, quarter * MAIN)
        kept_ref[part, :D] = in_ref[quarters[i], :MAIN, :].reshape(quarter * MAIN, D)
        kept_ref[part, D : 2 * D] = in_ref[quarters[i], MAIN : 2 * MAIN, :].reshape(quarter * MAIN, D)
    tail = in_ref[:, 2 * MAIN :, :].astype(F32).reshape(ENDS, D).astype(BF)
    kept_ref[WHOLE:, :D] = dot(ends_of(1, 0), tail).astype(BF)
    kept_ref[WHOLE:, D : 2 * D] = dot(ends_of(1, TAIL), tail).astype(BF)
    send(kept_ref.at[:, : 2 * D], kept_hbm.at[:, : 2 * D])
    rows = kept_ref[:, :D]
    rest = dot(rows, rest_ref[...])
    gate_pre = jnp.concatenate([dot(rows, gate_ref[:, :wide]), rest[:, :narrow]], axis=1)
    up_pre = jnp.concatenate([dot(rows, up_ref[:, :wide]), rest[:, narrow:]], axis=1)
    hidden_grad = dot(kept_ref[:, D : 2 * D], down_ref[...])
    sigma = jax.nn.sigmoid(gate_pre)
    silu = gate_pre * sigma
    gate_grad = (hidden_grad * up_pre * (sigma * (1.0 + gate_pre * (1.0 - sigma)))).astype(BF)
    up_grad = (hidden_grad * silu).astype(BF)
    hidden = (silu * up_pre).astype(BF)
    for i, value in enumerate((gate_grad, up_grad, hidden)):
        kept_ref[:, 2 * D + i * FF : 2 * D + (i + 1) * FF] = value
    send(kept_ref.at[:, 2 * D :], kept_hbm.at[:, 2 * D :])
    rest = jnp.concatenate([gate_grad[:, wide:], up_grad[:, wide:]], axis=1)
    for h in range(2):
        part = pl.ds(h * HALF, HALF)
        output = dot_cols(hidden, down_ref[part, :])
        input_grad = dot_cols(gate_grad[:, :wide], gate_ref[part, :wide])
        input_grad += dot_cols(up_grad[:, :wide], up_ref[part, :wide])
        input_grad = (input_grad + dot_cols(rest, rest_ref[part, :])).astype(BF)
        output = output.astype(BF)
        ends = dot(ends_of(0, 0), output[WHOLE:]) + dot(ends_of(0, TAIL), input_grad[WHOLE:])
        out_ref[:, h, :MAIN, :] = output[:WHOLE].reshape(EXPERTS, MAIN, HALF)
        out_ref[:, h, MAIN : 2 * MAIN, :] = input_grad[:WHOLE].reshape(EXPERTS, MAIN, HALF)
        out_ref[:, h, 2 * MAIN :, :] = ends.reshape(EXPERTS, 2 * TAIL, HALF).astype(BF)
        send(out_ref.at[:, h], out_hbm.at[:, h])
    for store in stores:
        store.wait()


def weights_body(kept_hbm, keep_ref, send_ref, kept_ref, all_ref, sems):
    core = lax.axis_index("dp") & 1
    rows, grads = pl.ds(0, D), pl.ds(2 * D, 2 * FF)
    back, hidden = pl.ds(D, D), pl.ds(2 * D + 2 * FF, FF)
    copies = [
        pltpu.make_async_copy(kept_hbm.at[:, part], kept_ref.at[:, part], sems.at[i])
        for i, part in enumerate((rows, grads, back, hidden))
    ]
    for copy in copies:
        copy.start()
    for copy in copies[:2]:
        copy.wait()
    both = dot_rows(kept_ref[:, rows], kept_ref[:, grads]).astype(BF)
    all_ref[:, :, : 2 * FF] = both.reshape(DEVS, GROUP, 2 * FF)
    for copy in copies[2:]:
        copy.wait()
    down = dot_rows(kept_ref[:, back], kept_ref[:, hidden]).astype(BF)
    all_ref[:, :, 2 * FF :] = down.reshape(DEVS, GROUP, FF)
    for i in range(RINGS):
        keep_ref[i] = all_ref[2 * i + core]
        send_ref[i] = all_ref[2 * i + 1 - core]


def around(z):
    return (z + 2 * (z & 1) - 1) & (RINGS - 1)


def add(left, right):
    return (left.astype(F32) + right.astype(F32)).astype(BF)


def split_body(keep_ref, got_ref, *outs):
    z = lax.axis_index("dp") >> 1
    half = GROUP // 2
    for part, (own, partner, later) in enumerate(((z, around(z), lambda i: i ^ 1), (z, z ^ 1, around))):
        rows = pl.ds(part * half, half)
        for ref, chip in zip(outs[2 * part : 2 * part + 2], (own, partner)):
            for i, chunk in enumerate((chip, chip ^ 4, later(chip), later(chip) ^ 4)):
                ref[i] = add(keep_ref[chunk, rows], got_ref[chunk, rows])


def halve_body(*refs):
    for mine_ref, got_ref, keep_ref, send_ref in (refs[0::2], refs[1::2]):
        half = mine_ref.shape[0] // 2
        keep_ref[...] = add(mine_ref[:half], got_ref[:half])
        send_ref[...] = add(mine_ref[half:], got_ref[half:])


def join_body(mine0_ref, mine1_ref, got0_ref, got1_ref, keep_ref, send_ref):
    half = GROUP // 2
    for part, (mine_ref, got_ref) in enumerate(((mine0_ref, got0_ref), (mine1_ref, got1_ref))):
        rows = pl.ds(part * half, half)
        keep_ref[0, rows] = add(mine_ref[0], got_ref[0])
        send_ref[0, rows] = add(mine_ref[1], got_ref[1])


def finish_body(own_ref, got_ref, gate_ref, up_ref, down_ref):
    total = add(own_ref[...], got_ref[...])
    gate_ref[...] = total[:, :, :FF]
    up_ref[...] = total[:, :, FF : 2 * FF]
    down_ref[...] = total[:, :, 2 * FF :]


def combine_body(ids_ref, gate_ref, back_ref, mixed_ref, grad_ref):
    places = home_places(ids_ref[...])
    gates = gate_ref[...]
    main_column = iota((TOK, WHOLE), 1).astype(F32)
    tail_column = iota((TOK, ENDS), 1).astype(F32)
    main = [jnp.zeros((TOK, WHOLE), F32)] * 2
    tail = [jnp.zeros((TOK, ENDS), F32)] * 2
    for k, (expert, place) in enumerate(places):
        gate = as_column(gates[k : k + 1, :])
        in_main = main_column == as_column(jnp.where(place < MAIN, expert * MAIN + place, -1))
        at = as_column(jnp.where(place < MAIN, -8, expert * 2 * TAIL + place - MAIN))
        main = [jnp.where(in_main, gate, main[0]), jnp.where(in_main, 1.0, main[1])]
        tail = [jnp.where(tail_column == at, gate, tail[0]), jnp.where(tail_column == at + TAIL, 1.0, tail[1])]

    def split(mix):
        high = mix.astype(BF)
        return high, (mix - high.astype(F32)).astype(BF)

    outs = [jnp.zeros((TOK, HALF), F32)] * 2
    for h in range(2):
        ends = back_ref[:, h, 2 * MAIN :, :].astype(F32).reshape(ENDS, HALF).astype(BF)
        output = back_ref[:, h, :MAIN, :].reshape(WHOLE, HALF)
        input_grad = back_ref[:, h, MAIN : 2 * MAIN, :].reshape(WHOLE, HALF)
        for part, rows in ((main, output), (tail, ends)):
            for piece in split(part[0]):
                outs[0] = outs[0] + dot(piece, rows)
        outs[1] = outs[1] + dot(main[1].astype(BF), input_grad) + dot(tail[1].astype(BF), ends)
    mixed_ref[...] = outs[0].astype(BF)
    grad_ref[...] = outs[1].astype(BF)


def runs():
    out, home = [], []
    device = lambda y, x, dp, high: ((4 * y + x) * DEVS + dp) * 2 + high
    for dp in range(DEVS):
        for start in (2 - 2 * (dp % 2), 6 - 2 * (dp % 2)):
            high = {(start + i) % 4: (start + i) % 8 // 4 for i in range(4)}
            out.append([device(y, x, dp, high[y]) for x in range(4) for y in range(4)])
        home.append([device(y, x, dp, high) for x in range(4) for y in range(4) for high in range(2)])
    return out, home


def along_z(value, target):
    return lax.ppermute(value, "dp", [(2 * z + core, 2 * (target(z) % RINGS) + core) for z in range(RINGS) for core in range(2)])


def sum_groups(keep, send):
    some = lambda count: shape(count, GROUP // 2, 3 * FF)
    whole = shape(1, GROUP, 3 * FF)
    got = lax.ppermute(send, "dp", [(i, i ^ 1) for i in range(DEVS)])
    mine0, other0, mine1, other1 = call(split_body, (some(4),) * 4, 10, 0, 12 * D * FF)(keep, got)
    got0, got1 = along_z(other0, around), along_z(other1, lambda z: z ^ 1)
    mine0, mine1, other0, other1 = call(halve_body, (some(2),) * 4, 10, 0, 6 * D * FF)(mine0, mine1, got0, got1)
    got0, got1 = along_z(other0, lambda z: z ^ 1), along_z(other1, around)
    mine, other = call(join_body, (whole, whole), 10, 0, 3 * D * FF)(mine0, mine1, got0, got1)
    got = along_z(other, lambda z: z ^ 4)
    return call(finish_body, (shape(1, GROUP, FF),) * 3, 10, 0, 2 * D * FF)(mine, got)


def local(tokens, expert_ids, gate_values, w_gate, w_up, w_down, cotangent):
    ids, gates = expert_ids.T, gate_values.T
    mm = 2 * ROWS * D * FF
    hbm, vmem = pl.BlockSpec(memory_space=pltpu.HBM), pl.BlockSpec(memory_space=pltpu.VMEM)
    chunks = call(
        place_body,
        shape(EXPERTS, CHUNK, D),
        61,
        4 * mm,
        8 * ROWS * D,
        [
            pltpu.VMEM((EXPERTS, CHUNK, D), BF),
            pltpu.VMEM((2, TOK), jnp.int32),
            pltpu.VMEM((2, TOK), F32),
            pltpu.VMEM((TOK, D), BF),
            pltpu.VMEM((TOK, D), BF),
            pltpu.SemaphoreType.DMA((6,)),
        ],
        in_specs=[hbm] * 4,
        out_specs=hbm,
    )(ids, gates, tokens, cotangent)
    everywhere = ("loop", "dp", "tensor")
    out_groups, home_groups = runs()
    arrived = lax.all_to_all(chunks, everywhere, 0, 0, tiled=True, axis_index_groups=out_groups)
    kept = shape(ROWS, 2 * D + 3 * FF)
    results, kept = call(
        expert_body,
        (shape(EXPERTS, 2, CHUNK, HALF), kept),
        50,
        6 * mm,
        16 * ROWS * D,
        [
            pltpu.VMEM((EXPERTS, CHUNK, D), BF),
            pltpu.VMEM((EXPERTS, 2, CHUNK, HALF), BF),
            pltpu.VMEM((ROWS, 2 * D + 3 * FF), BF),
            pltpu.VMEM((D, 256), BF),
            pltpu.SemaphoreType.DMA((8,)),
        ],
        in_specs=[hbm, vmem, vmem, vmem],
        out_specs=(hbm, hbm),
    )(arrived, w_gate[0], w_up[0], w_down[0])
    home = lax.all_to_all(
        results.reshape(2 * EXPERTS, CHUNK, HALF), everywhere, 0, 0, tiled=True, axis_index_groups=home_groups
    ).reshape(EXPERTS, 2, CHUNK, HALF)
    keep, send = call(
        weights_body,
        (shape(RINGS, GROUP, 3 * FF), shape(RINGS, GROUP, 3 * FF)),
        50,
        3 * mm,
        8 * ROWS * D,
        [
            pltpu.VMEM((ROWS, 2 * D + 3 * FF), BF),
            pltpu.VMEM((DEVS, GROUP, 3 * FF), BF),
            pltpu.SemaphoreType.DMA((4,)),
        ],
        in_specs=[hbm],
    )(kept)
    grads = sum_groups(keep, send)
    mixed, token_grad = call(combine_body, (shape(TOK, HALF), shape(TOK, HALF)), 16, 2 * mm, 8 * ROWS * D)(
        ids, gates, home
    )
    return (mixed, token_grad, *grads)


def solution(mesh):
    spread = P(("loop", "dp"), None)
    weight = P("loop", None, "tensor")
    return jax.shard_map(
        local,
        mesh=mesh,
        in_specs=(spread, spread, spread, weight, weight, weight, spread),
        out_specs=(P(("loop", "dp"), "tensor"),) * 2 + (P("loop", "dp", "tensor"),) * 3,
        check_vma=False,
    )
```
